1024 devices in a mesh: grp: 16 (over x, core), mem: 64 (over y, z).
Axes of the slice: x: 8, y: 8, z: 8, core: 2. Of those that a mesh axis runs over, the one named last changes fastest.
Arguments:
- embeddings: bfloat16 [524288, 1024], P(('grp', 'mem')), may hold values from -6 to 6
- assignment: int32 [524288], P(('grp', 'mem')), may hold values from 0 to 131071, as said below
- second_choice: int32 [524288], P(('grp', 'mem')), may hold values from 0 to 131071, as said below
- list_slot: int32 [131072], replicated, may hold values from 0 to 131071, as said below
- old_centroids: bfloat16 [131072, 1024], P(('grp', 'mem')), may hold values from -6 to 6
Outputs:
- new_centroids: bfloat16 [131072, 1024], P(('grp', 'mem'))
- margins: float32 [524288], P(('grp', 'mem'))
The draws below stay inside these ranges and needn't reach their ends.
Inputs may be any that keep to these rules, and one draw needn't show every extreme that they name: Each list is stored at slot list_slot[list]; the slots are a permutation of all lists. Slot s lies on device s // 128 in the order grp then mem. `assignment`: of the 512 vectors of one device, at most 10 have a list whose slot lies on one index of mem (any grp); every device has one index of mem that receives exactly 10. `second_choice`: A vector's second-choice list differs from its list, and its slot lies on the same index of mem as the slot of its list.
All inputs are finite; a program needn't handle non-finite values.
Results may differ from the reference program's by a relative error of at most 0.015.
Values may be sent and summed in bfloat16 or wider, within the bound.
No kernel may reach another device: no remote copies, remote signals or barrier semaphores. Data moves between devices by JAX's collectives and lax.ppermute only.
A program may use at most 32 MiB of HBM per device.

```python
import jax
import jax.numpy as jnp
from jax import lax

D = 1024
LISTS_DEV = 128
V_DEV = 512
CAP = 10
VECTORS = 524288
LISTS = 131072
N_GRP = 16
N_MEM = 64


def shared_order(key):
    return jax.random.permutation(key, LISTS_DEV * N_GRP * N_MEM).astype(jnp.int32)


def inverse_order(key):
    order = shared_order(key)
    return jnp.zeros_like(order).at[order].set(jnp.arange(order.shape[0], dtype=jnp.int32))


def first_parts(key):
    key = jax.random.fold_in(key, 11)
    devices = N_GRP * N_MEM
    positions = N_MEM * CAP
    span = N_GRP * LISTS_DEV
    keys = jax.random.split(key, 7)
    noise = jax.random.randint(keys[0], (devices, positions), 0, 2 ** 14)
    heavy = jax.random.randint(keys[1], (N_MEM,), 0, 4)
    owner_of = jnp.arange(positions, dtype=jnp.int32) // CAP
    hot = jax.random.randint(keys[2], (devices,), 0, N_MEM)
    score = noise + heavy[owner_of][None, :] * 2 ** 13
    score = score + jnp.where(owner_of[None, :] == hot[:, None], 2 ** 17, 0)
    distinct = score * positions + jnp.arange(positions, dtype=jnp.int32)[None, :]
    _, chosen = lax.top_k(distinct, V_DEV)
    chosen = jax.random.permutation(keys[3], chosen, axis=1, independent=True)
    owner = (chosen // CAP).astype(jnp.int32)
    within = (chosen % CAP).astype(jnp.int32)
    device_ids = jnp.arange(devices, dtype=jnp.int32)
    sender_mem = (device_ids % N_MEM)[:, None]
    sender_grp = (device_ids // N_MEM)[:, None]
    spot = (sender_mem * CAP + within) % span
    perm_keys = jax.random.split(keys[4], devices)
    tables = jax.vmap(lambda k: jax.random.permutation(k, span).astype(jnp.int32))(perm_keys)
    picked = tables[sender_grp * N_MEM + owner, spot]
    wild = jax.random.randint(keys[5], (devices, V_DEV), 0, span)
    redraw = jax.random.randint(keys[6], (devices, V_DEV), 0, 8) == 0
    picked = jnp.where(redraw, wild, picked)
    group = (picked // LISTS_DEV).astype(jnp.int32)
    local = (picked % LISTS_DEV).astype(jnp.int32)
    return (group, owner, local)


def draw_list_slot(key, part):
    return shared_order(key)


def draw_assignment(key, part):
    inverse = inverse_order(key)
    group, owner, local = first_parts(key)
    slot = (group * N_MEM + owner) * LISTS_DEV + local
    return inverse[slot.reshape(-1)].astype(jnp.int32)


def draw_second_choice(key, part):
    inverse = inverse_order(key)
    group, owner, local = first_parts(key)
    key = jax.random.fold_in(key, 12)
    keys = jax.random.split(key, 2)
    other_group = jax.random.randint(keys[0], group.shape, 0, N_GRP)
    other_local = jax.random.randint(keys[1], group.shape, 0, LISTS_DEV)
    clash = (other_group == group) & (other_local == local)
    other_local = jnp.where(clash, (local + 1) % LISTS_DEV, other_local)
    slot = (other_group * N_MEM + owner) * LISTS_DEV + other_local
    return inverse[slot.reshape(-1)].astype(jnp.int32)


def shard_levels(own_key, shape, shards, smallest, largest):
    def one(axis_at, blocks):
        steps = jax.random.uniform(jax.random.fold_in(jax.random.fold_in(own_key, 6), axis_at), (blocks,), jnp.float32, smallest / len(shards), largest / len(shards))
        return jnp.repeat(jnp.exp(steps), shape[axis_at] // blocks).reshape((-1,) + (1,) * (len(shape) - axis_at - 1))

    factor_of = one(*shards[0])
    for cut in shards[1:]:
        factor_of = factor_of * one(*cut)
    return factor_of


def centred(own_key, dims, deviation, limit, shards=(), kind=jnp.bfloat16):
    drawn = jax.random.normal(own_key, dims, jnp.float32) * deviation
    if len(shards) > 0:
        drawn = shard_levels(own_key, dims, shards, -0.22, 0.18) * drawn
    return jnp.clip(drawn, min=-limit, max=limit).astype(kind)


def setup_inputs(seed: int = 0) -> dict:
    key_of = jax.random.split(jax.random.key(seed), 6)
    embeddings = centred(key_of[0], (VECTORS, D), 1.0, 6.0, ((0, 1024),))
    assignment = draw_assignment(jax.random.fold_in(key_of[5], 71), 0)
    second_choice = draw_second_choice(jax.random.fold_in(key_of[5], 71), 0)
    list_slot = draw_list_slot(jax.random.fold_in(key_of[5], 71), 0)
    old_centroids = centred(key_of[4], (LISTS, D), 1.0, 6.0, ((0, 1024),))
    return {"embeddings": embeddings, "assignment": assignment, "second_choice": second_choice, "list_slot": list_slot, "old_centroids": old_centroids}


def reference(embeddings, assignment, second_choice, list_slot, old_centroids):
    first_slot = list_slot[assignment]
    second_slot = list_slot[second_choice]
    rows_group = V_DEV * N_MEM
    group_rows = embeddings.reshape(N_GRP, rows_group, D)
    group_slots = first_slot.reshape(N_GRP, rows_group)

    def add_group(total, items):
        rows, slots = items
        part = jnp.zeros((LISTS, D), jnp.float32).at[slots].add(rows.astype(jnp.float32))
        rounded = lax.optimization_barrier(part.astype(jnp.bfloat16))
        return total + rounded.astype(jnp.float32), None

    summed, _ = lax.scan(add_group, jnp.zeros((LISTS, D), jnp.float32), (group_rows, group_slots))
    counts = jnp.zeros((LISTS,), jnp.float32).at[first_slot].add(1.0)
    fresh = ((summed + old_centroids.astype(jnp.float32)) / (counts + 1.0)[:, None]).astype(jnp.bfloat16)
    values = embeddings.astype(jnp.float32)
    near = fresh[first_slot].astype(jnp.float32)
    other = fresh[second_slot].astype(jnp.float32)
    margins = (jnp.sum((values - other) ** 2, axis=1) - jnp.sum((values - near) ** 2, axis=1)) / D
    return fresh, margins
```

```python
import functools

import jax
import jax.numpy as jnp
from jax import lax
from jax.experimental import pallas as pl
from jax.experimental.pallas import tpu as pltpu
from jax.sharding import Mesh
from jax.sharding import PartitionSpec as P

F32 = jnp.float32
BF16 = jnp.bfloat16
LANES = 128
ID_ROWS = 8
PARAMS = pltpu.CompilerParams(vmem_limit_bytes=56 * 2**20)


def rows_of(shape):
    return lax.broadcasted_iota(jnp.int32, shape, 0).astype(F32)


def lanes_of(shape):
    return lax.broadcasted_iota(jnp.int32, shape, 1).astype(F32)


def hot(condition):
    return jnp.where(condition, 1.0, 0.0).astype(BF16)


def dot(a, b, contract):
    return lax.dot_general(a, b, (contract, ((), ())), preferred_element_type=F32)


def prepare(members, capacity, first, second, table, embeddings, packed, labels, place):
    vectors = first.shape[1]
    slots = table[...]
    local = slots & (LANES - 1)
    owner = (slots // LANES) & (members - 1)
    group = slots // (LANES * members)
    planes = jnp.concatenate([local, owner, group], axis=1).astype(F32).astype(BF16)

    def look_up(ids):
        row = (ids // LANES).astype(F32)
        lane = (ids & (LANES - 1)).astype(F32)
        found = dot(planes, hot(rows_of((table.shape[0], vectors)) == row), ((0,), (0,)))
        mask = rows_of((LANES, vectors)) == lane

        def pick(k):
            return jnp.sum(
                jnp.where(mask, found[k * LANES : (k + 1) * LANES], 0.0), axis=0, keepdims=True
            )

        return pick(0), pick(1), pick(2)

    first_local, first_owner, first_group = look_up(first[...])
    second_local, _, second_group = look_up(second[...])
    is_owner = rows_of((members, vectors)) == first_owner
    before = hot(rows_of((vectors, vectors)) < lanes_of((vectors, vectors)))
    earlier = dot(hot(is_owner), before, ((1,), (0,)))
    rank = jnp.sum(jnp.where(is_owner, earlier, 0.0), axis=0, keepdims=True)
    spot = first_owner * capacity + rank
    order = hot(rows_of((members * capacity, vectors)) == spot)
    packed[...] = dot(order, embeddings[...], ((1,), (0,))).astype(BF16)
    ranked = rows_of((16, vectors)) == rank
    digits = [first_group + 1.0, first_local, second_group + 1.0, second_local]
    spread = [jnp.where(ranked, digit, 0.0) for digit in digits]
    spread.append(jnp.zeros((LANES - 16 * len(digits), vectors), F32))
    table_of = jnp.concatenate(spread, axis=0).astype(BF16)
    labels[...] = dot(hot(is_owner), table_of, ((1,), (1,))).astype(BF16)
    place[...] = spot.astype(jnp.int32)


def partial_sums(
    chips, capacity, where, own, other, own_labels, other_labels, ids, *blocks
):
    chip = where[0].astype(F32)
    core = where[1].astype(F32)
    members = own_labels.shape[0]
    count = own.shape[0]
    width = own.shape[1]
    from_member = jnp.floor((lanes_of((members, count)) + 0.5) * (1.0 / capacity))
    spread = hot(rows_of((members, count)) == from_member)
    position = lanes_of((16, count))
    position = position - capacity * jnp.floor((position + 0.5) * (1.0 / capacity))
    ranked = rows_of((16, count)) == position

    def decode(labels):
        found = dot(labels[...], spread, ((0,), (0,)))

        def pick(k):
            return jnp.sum(
                jnp.where(ranked, found[k * 16 : (k + 1) * 16], 0.0), axis=0, keepdims=True
            )

        def index(group, local):
            group = group - 1.0
            at_chip = jnp.floor((group + 0.5) * 0.5)
            at_core = group - 2.0 * at_chip
            ahead = at_chip - chip
            ahead = jnp.where(ahead < 0.0, ahead + chips, ahead)
            mine = (group >= 0.0) & (at_core == core)
            return jnp.where(mine, ahead * LANES + local, -1.0)

        return index(pick(0), pick(1)), index(pick(2), pick(3))

    own_first, own_second = decode(own_labels)
    other_first, other_second = decode(other_labels)
    first = jnp.concatenate([own_first, other_first], axis=1)
    second = jnp.concatenate([own_second, other_second], axis=1)
    ids[0:1, :] = first
    ids[1:2, :] = second
    ones = jnp.ones((16, 2 * count), BF16)
    for ahead in range(chips):
        table = hot(rows_of((LANES, 2 * count)) + ahead * LANES == first)
        total = dot(table[:, :count], own[...], ((1,), (0,))) + dot(
            table[:, count:], other[...], ((1,), (0,))
        )
        hits = dot(ones, table, ((1,), (1,)))
        high = jnp.floor(hits * (1.0 / 256.0))
        rest = hits - 256.0 * high
        middle = jnp.floor(rest * (1.0 / 16.0))
        low = rest - 16.0 * middle
        block = blocks[ahead]
        block[0:LANES, :] = total.astype(BF16)
        block[LANES : LANES + 16, :] = jnp.concatenate(
            [low, middle, high, jnp.zeros((16, width - 3 * LANES), F32)], axis=1
        ).astype(BF16)


def refit(mine, above, below, old, fresh):
    total = mine[...].astype(F32) + above[...].astype(F32) + below[...].astype(F32)
    digits = total[LANES : LANES + 16].astype(BF16)
    identity = hot(rows_of((LANES, LANES)) == lanes_of((LANES, LANES)))

    def column(k):
        return dot(identity, digits[:, k * LANES : (k + 1) * LANES], ((1,), (1,)))[:, 0:1]

    counts = column(0) + 16.0 * column(1) + 256.0 * column(2)
    fresh[...] = ((total[0:LANES] + old[...].astype(F32)) / (counts + 1.0)).astype(BF16)


def score(chips, own, other, ids, *refs):
    blocks, out = refs[:-1], refs[-1]
    width = own.shape[1]
    count = own.shape[0]
    first = ids[0:1, :]
    second = ids[1:2, :]
    total = jnp.zeros((1, 2 * count), F32)
    for ahead in range(chips):
        block = blocks[ahead][...]
        products = [dot(block, v[...], ((1,), (1,))) for v in (own, other)]
        product = jnp.concatenate(products, axis=1)
        size = jnp.sum(block.astype(F32) ** 2, axis=1, keepdims=True)
        distance = size - 2.0 * product
        at = rows_of((LANES, 2 * count)) + ahead * LANES
        total += jnp.sum(
            jnp.where(at == second, distance, 0.0) - jnp.where(at == first, distance, 0.0),
            axis=0,
            keepdims=True,
        )
    out[...] = total * (1.0 / width)


def shifted(axis, size, step):
    pairs = [(i, (i + step) % size) for i in range(size)]
    return lambda a: lax.ppermute(a, axis, pairs)


def add(a, b):
    return (a.astype(F32) + b.astype(F32)).astype(BF16)


def ring_sum(up, down, blocks):
    half = blocks[0].shape[1] // 2
    above = up(blocks[4][:, :half])
    below = down(blocks[4][:, half:])
    above = up(jnp.concatenate([add(blocks[3][:, :half], above), blocks[3][:, half:]], axis=1))
    below = down(jnp.concatenate([blocks[5][:, :half], add(blocks[5][:, half:], below)], axis=1))
    above = up(add(blocks[2], above))
    below = down(add(blocks[6], below))
    above = up(add(blocks[1], above))
    below = down(add(blocks[7], below))
    return blocks[0], above, below


def ring_gather(up, down, block):
    half = block.shape[1] // 2
    above, below = [block], [block]
    for _ in range(3):
        above.append(up(above[-1]))
        below.append(down(below[-1]))
    far = jnp.concatenate([up(above[3][:, :half]), down(below[3][:, half:])], axis=1)
    return [block, below[1], below[2], below[3], far, above[3], above[2], above[1]]


def on_device(embeddings, assignment, second_choice, list_slot, old_centroids):
    vectors, width = embeddings.shape
    lists = old_centroids.shape[0]
    members = lax.axis_size("mem")
    chips = lax.axis_size("x")
    capacity = vectors // members + 2
    count = members * capacity
    tiles = capacity * width // LANES
    up = shifted("x", chips, 1)
    down = shifted("x", chips, -1)
    across = shifted("core", 2, 1)

    packed, labels, place = pl.pallas_call(
        functools.partial(prepare, members, capacity),
        out_shape=(
            jax.ShapeDtypeStruct((count, width), BF16),
            jax.ShapeDtypeStruct((members, LANES), BF16),
            jax.ShapeDtypeStruct((1, vectors), jnp.int32),
        ),
        compiler_params=PARAMS,
        name="prepare",
    )(
        assignment.reshape(1, vectors),
        second_choice.reshape(1, vectors),
        list_slot.reshape(-1, LANES),
        embeddings,
    )
    outgoing = jnp.concatenate(
        [
            packed.reshape(members, tiles, LANES),
            jnp.pad(labels[:, None, :], ((0, 0), (0, ID_ROWS - 1), (0, 0))),
        ],
        axis=1,
    )
    arrived = lax.all_to_all(outgoing, "mem", split_axis=0, concat_axis=0, tiled=True)
    beside = across(arrived)

    def unpack(a):
        return a[:, :tiles].reshape(count, width), a[:, tiles]

    own, own_labels = unpack(arrived)
    other, other_labels = unpack(beside)
    where = jnp.stack([lax.axis_index("x"), lax.axis_index("core")]).astype(jnp.int32)
    vmem = pl.BlockSpec(memory_space=pltpu.VMEM)
    ids, *blocks = pl.pallas_call(
        functools.partial(partial_sums, chips, capacity),
        in_specs=[pl.BlockSpec(memory_space=pltpu.SMEM)] + [vmem] * 4,
        out_shape=[jax.ShapeDtypeStruct((2, 2 * count), F32)]
        + [jax.ShapeDtypeStruct((lists + 16, width), BF16)] * chips,
        compiler_params=PARAMS,
        name="partial_sums",
    )(where, own, other, own_labels, other_labels)
    fresh = pl.pallas_call(
        refit,
        out_shape=jax.ShapeDtypeStruct((lists, width), BF16),
        compiler_params=PARAMS,
        name="refit",
    )(*ring_sum(up, down, blocks), old_centroids)
    scored = pl.pallas_call(
        functools.partial(score, chips),
        out_shape=jax.ShapeDtypeStruct((1, 2 * count), F32),
        compiler_params=PARAMS,
        name="score",
    )(own, other, ids, *ring_gather(up, down, fresh))
    scored = scored.reshape(2, members, 1, capacity)
    margin = scored[0] + across(scored[1])
    returned = lax.all_to_all(margin, "mem", split_axis=0, concat_axis=0, tiled=True)
    spots = jnp.arange(count, dtype=jnp.int32)
    margins = jnp.sum(
        jnp.where(place.reshape(vectors, 1) == spots[None, :], returned.reshape(1, count), 0.0),
        axis=1,
    )
    return fresh, margins


def solution(mesh):
    groups, members = mesh.devices.shape
    chip_mesh = Mesh(mesh.devices.reshape(groups // 2, 2, members), ("x", "core", "mem"))
    everywhere = ("x", "core", "mem")
    placed = (
        P(everywhere, None),
        P(everywhere),
        P(everywhere),
        P(),
        P(everywhere, None),
    )
    return jax.shard_map(
        on_device,
        mesh=chip_mesh,
        in_specs=placed,
        out_specs=(P(everywhere, None), P(everywhere)),
        check_vma=False,
    )
```

```python
import functools

import jax
import jax.numpy as jnp
from jax import lax
from jax.experimental import pallas as pl
from jax.experimental.pallas import tpu as pltpu
from jax.sharding import Mesh
from jax.sharding import PartitionSpec as P

F32 = jnp.float32
BF16 = jnp.bfloat16
LANES = 128
TILE = 8
NOTES = 16
SMEM = pl.BlockSpec(memory_space=pltpu.SMEM)
VMEM = pl.BlockSpec(memory_space=pltpu.VMEM)


def rows_of(shape):
    return lax.broadcasted_iota(jnp.int32, shape, 0).astype(F32)


def lanes_of(shape):
    return lax.broadcasted_iota(jnp.int32, shape, 1).astype(F32)


def hot(condition):
    return jnp.where(condition, 1.0, 0.0).astype(BF16)


def dot(a, b, contract):
    return lax.dot_general(a, b, (contract, ((), ())), preferred_element_type=F32)


def whole(a, size):
    return jnp.floor((a + 0.5) * (1.0 / size))


def call(kernel, name, out_shape, flops, *args, scalars=None):
    specs = [VMEM] * len(args)
    if scalars is not None:
        specs = [SMEM] + specs
        args = (scalars,) + args
    return pl.pallas_call(
        kernel,
        in_specs=specs,
        out_shape=out_shape,
        compiler_params=pltpu.CompilerParams(vmem_limit_bytes=56 * 2**20),
        cost_estimate=pl.CostEstimate(flops=flops, bytes_accessed=2**21, transcendentals=0),
        name=name,
    )(*args)


def prepare(members, capacity, first, second, table, embeddings, payload, place):
    vectors = first.shape[1]
    parts = embeddings.shape[1] // LANES
    slots = table[...]
    local = slots & (LANES - 1)
    owner = (slots // LANES) & (members - 1)
    group = slots // (LANES * members)
    planes = jnp.concatenate([local, owner, group], axis=1).astype(F32).astype(BF16)

    def look_up(ids):
        row = (ids // LANES).astype(F32)
        lane = (ids & (LANES - 1)).astype(F32)
        found = dot(planes, hot(rows_of((table.shape[0], vectors)) == row), ((0,), (0,)))
        mask = rows_of((LANES, vectors)) == lane

        def pick(k):
            return jnp.sum(
                jnp.where(mask, found[k * LANES : (k + 1) * LANES], 0.0), axis=0, keepdims=True
            )

        return pick(0), pick(1), pick(2)

    first_local, first_owner, first_group = look_up(first[...])
    second_local, _, second_group = look_up(second[...])
    is_owner = rows_of((members, vectors)) == first_owner
    before = hot(rows_of((vectors, vectors)) < lanes_of((vectors, vectors)))
    earlier = dot(hot(is_owner), before, ((1,), (0,)))
    rank = jnp.sum(jnp.where(is_owner, earlier, 0.0), axis=0, keepdims=True)
    place[...] = (first_owner * capacity + rank).astype(jnp.int32)
    spot = jnp.where(
        rank < TILE, first_owner * TILE + rank, rank * members + first_owner
    )
    order = hot(rows_of((members * capacity, vectors)) == spot)
    packed = dot(order, embeddings[...], ((1,), (0,)))
    pieces = [
        packed[: TILE * members, j * LANES : (j + 1) * LANES].reshape(members, TILE, LANES)
        for j in range(parts)
    ]
    for p in range(TILE, capacity):
        vector = packed[p * members : (p + 1) * members]
        pieces.append(
            jnp.stack([vector[:, j * LANES : (j + 1) * LANES] for j in range(parts)], axis=1)
        )
    ranked = rows_of((16, vectors)) == rank
    digits = [first_group + 1.0, first_local, second_group + 1.0, second_local]
    spread = [jnp.where(ranked, digit, 0.0) for digit in digits]
    spread.append(jnp.zeros((LANES - 16 * len(digits), vectors), F32))
    labels = dot(
        hot(is_owner), jnp.concatenate(spread, axis=0).astype(BF16), ((1,), (1,))
    )
    pieces.append(jnp.broadcast_to(labels[:, None, :], (members, TILE, LANES)))
    payload[...] = jnp.concatenate(pieces, axis=1).astype(BF16)


def unpack(capacity, arrived, box):
    members = arrived.shape[0]
    count = members * capacity
    width = box.shape[1]
    parts = width // LANES
    values = arrived[...].astype(F32)
    for j in range(parts):
        at = slice(j * LANES, (j + 1) * LANES)
        box[: TILE * members, at] = (
            values[:, j * TILE : (j + 1) * TILE].reshape(TILE * members, LANES).astype(BF16)
        )
        for p in range(TILE, capacity):
            box[p * members : (p + 1) * members, at] = values[:, p * parts + j].astype(BF16)
    labels = values[:, capacity * parts].astype(BF16)
    vector = lanes_of((members, count))
    from_member = jnp.where(
        vector < TILE * members, whole(vector, TILE), vector - members * whole(vector, members)
    )
    found = dot(labels, hot(rows_of((members, count)) == from_member), ((0,), (0,)))
    vector = lanes_of((16, count))
    rank = jnp.where(
        vector < TILE * members, vector - TILE * whole(vector, TILE), whole(vector, members)
    )
    ranked = rows_of((16, count)) == rank
    rows = [
        jnp.sum(jnp.where(ranked, found[k * 16 : (k + 1) * 16], 0.0), axis=0, keepdims=True)
        for k in range(4)
    ]
    notes = jnp.concatenate(rows + [jnp.zeros((NOTES - 4, count), F32)], axis=0)
    notes = jnp.concatenate([notes, jnp.zeros((NOTES, width - count), F32)], axis=1)
    box[count : count + NOTES] = notes.astype(BF16)


def index(chips, where, notes, k, towards):
    chip = where[0].astype(F32)
    core = where[1].astype(F32)
    group = notes[2 * k : 2 * k + 1] - 1.0
    local = notes[2 * k + 1 : 2 * k + 2]
    at_chip = whole(group, 2)
    at_core = group - 2.0 * at_chip
    way = 1.0 - 2.0 * core
    away = (at_chip - chip) * (way if towards else -way)
    away = away - chips * jnp.floor((away + 0.5) * (1.0 / chips))
    return jnp.where(group >= 0.0, away * (2 * LANES) + at_core * LANES + local, -1.0)


def halves(where, width):
    half = width // 2
    core = where[1]
    return (
        pl.ds(pl.multiple_of(core * half, half), half),
        pl.ds(pl.multiple_of((1 - core) * half, half), half),
    )


def sums(chips, count, added, where, box, *refs):
    earlier, outs = refs[: len(refs) - 5], refs[-5:]
    width = box.shape[1]
    half = width // 2
    lists = 2 * LANES
    notes = box[count : count + NOTES, :count].astype(F32)
    at = index(chips, where, notes, 0, True)
    mine, rest = halves(where, width)
    ones = jnp.ones((NOTES, count), BF16)
    for k in range(5):
        table = hot(rows_of((lists, count)) + k * lists == at)
        hits = dot(ones, table, ((1,), (1,)))
        high = whole(hits, 256)
        left = hits - 256.0 * high
        middle = whole(left, 16)
        low = left - 16.0 * middle
        one = jnp.concatenate([low, middle], axis=1)
        two = jnp.concatenate([high, jnp.zeros((NOTES, half - lists), F32)], axis=1)
        digits = [jnp.where(where[1] == 0, one, two), jnp.where(where[1] == 0, two, one)]
        for n, columns in enumerate([mine] if k in (0, 4) else [mine, rest]):
            total = jnp.concatenate(
                [dot(table, box[0:count, columns], ((1,), (0,))), digits[n]], axis=0
            )
            to = slice(n * half, (n + 1) * half)
            if added:
                total = total + earlier[k][:, to].astype(F32)
            outs[k][:, to] = total.astype(BF16)


def refit(where, here, there, old, other_old, turned, fresh):
    width = here.shape[1]
    half = width // 2
    lists = 2 * LANES
    first = where[1] == 0
    left = here[:, :half].astype(F32) + there[:, half:].astype(F32)
    right = here[:, half:].astype(F32) + there[:, :half].astype(F32)

    def order(a, b):
        return jnp.where(first, a, b), jnp.where(first, b, a)

    one, two = order(left[lists:], right[lists:])
    identity = hot(rows_of((lists, lists)) == lanes_of((lists, lists)))

    def column(digits):
        return dot(identity, digits.astype(BF16), ((1,), (1,)))[:, 0:1]

    counts = column(one[:, :lists]) + 16.0 * column(one[:, lists : 2 * lists])
    counts = counts + 256.0 * column(two[:, :lists]) + 1.0
    both = jnp.concatenate(order(old[...].astype(F32), other_old[...].astype(F32)), axis=0)
    old_left, old_right = order(both[:, :half], both[:, half:])
    left = (left[:lists] + old_left) / counts
    right = (right[:lists] + old_right) / counts
    turned[:, :half] = left.astype(BF16)
    turned[:, half:] = right.astype(BF16)
    one, two = order(left, right)
    fresh[:, :half] = order(one[:LANES], one[LANES:])[0].astype(BF16)
    fresh[:, half:] = order(two[:LANES], two[LANES:])[0].astype(BF16)


def score(chips, count, k, where, own, other, block, *refs):
    before, out = refs[:-1], refs[-1]
    lists = block.shape[0]
    half = own.shape[1] // 2
    mine, rest = halves(where, own.shape[1])
    values = block[...]
    size = jnp.sum(values.astype(F32) ** 2, axis=1, keepdims=True)
    for n, box in enumerate((own, other)):
        notes = box[count : count + NOTES, :count].astype(F32)
        product = dot(values[:, :half], box[0:count, mine], ((1,), (1,)))
        if block.shape[1] > half:
            product = product + dot(values[:, half:], box[0:count, rest], ((1,), (1,)))
        distance = size - 2.0 * product
        at = rows_of((lists, count)) + k * lists
        is_first = at == index(chips, where, notes, 0, False)
        is_second = at == index(chips, where, notes, 1, False)
        total = jnp.sum(
            jnp.where(is_second, distance, 0.0) - jnp.where(is_first, distance, 0.0),
            axis=0,
            keepdims=True,
        )
        if before:
            total = total + before[0][n : n + 1]
        out[n : n + 1] = total


def add(a, b):
    return (a.astype(F32) + b.astype(F32)).astype(BF16)


def on_device(embeddings, assignment, second_choice, list_slot, old_centroids):
    vectors, width = embeddings.shape
    lists = old_centroids.shape[0]
    members = lax.axis_size("mem")
    chips = lax.axis_size("x")
    capacity = vectors // members + 2
    count = members * capacity
    half = width // 2
    tiles = (capacity + 1) * TILE
    around = [(2 * i, 2 * ((i + 1) % chips)) for i in range(chips)]
    around += [(2 * i + 1, 2 * ((i - 1) % chips) + 1) for i in range(chips)]

    def onward(a):
        return lax.ppermute(a, ("x", "core"), around)

    def across(a):
        return lax.ppermute(a, "core", [(0, 1), (1, 0)])

    def shape(*dims, kind=BF16):
        return jax.ShapeDtypeStruct(dims, kind)

    where = jnp.stack([lax.axis_index("x"), lax.axis_index("core")]).astype(jnp.int32)
    payload, place = call(
        functools.partial(prepare, members, capacity),
        "prepare",
        (shape(members, tiles, LANES), shape(1, vectors, kind=jnp.int32)),
        2**31,
        assignment.reshape(1, vectors),
        second_choice.reshape(1, vectors),
        list_slot.reshape(-1, LANES),
        embeddings,
    )
    arrived = lax.all_to_all(payload, "mem", split_axis=0, concat_axis=0, tiled=True)
    own = call(
        functools.partial(unpack, capacity), "unpack", shape(count + NOTES, width), 2**24, arrived
    )
    other = across(own)
    other_old = across(old_centroids)
    rows = 2 * lists + NOTES
    widths = (half, width, width, width, half)
    sums_shape = [shape(rows, w) for w in widths]
    flops = 2**31
    blocks = call(
        functools.partial(sums, chips, count, False), "sums", sums_shape, flops, own, scalars=where
    )
    near, one, two, three, far = call(
        functools.partial(sums, chips, count, True),
        "sums",
        sums_shape,
        flops,
        other,
        *blocks,
        scalars=where,
    )
    moving = onward(far)
    moving = onward(jnp.concatenate([add(three[:, :half], moving), three[:, half:]], axis=1))
    moving = onward(add(two, moving))
    moving = onward(add(one, moving))
    here = jnp.concatenate([add(near, moving[:, :half]), moving[:, half:]], axis=1)
    turned, fresh = call(
        refit,
        "refit",
        (shape(2 * lists, width), shape(lists, width)),
        2**24,
        here,
        across(here),
        old_centroids,
        other_old,
        scalars=where,
    )

    def scored(k, block, *before):
        return call(
            functools.partial(score, chips, count, k),
            "score",
            shape(2, count, kind=F32),
            2**31,
            own,
            other,
            block,
            *before,
            scalars=where,
        )

    first = onward(turned)
    total = scored(0, turned[:, :half])
    second = onward(first)
    total = scored(1, first, total)
    third = onward(second)
    total = scored(2, second, total)
    fourth = onward(third[:, :half])
    total = scored(3, third, total)
    total = scored(4, fourth, total)
    margin = (total[0] + across(total[1])) * (1.0 / width)
    margin = jnp.concatenate(
        [
            margin[: TILE * members].reshape(members, TILE),
            margin[TILE * members :].reshape(capacity - TILE, members).T,
        ],
        axis=1,
    )
    returned = lax.all_to_all(
        margin.reshape(members, 1, capacity), "mem", split_axis=0, concat_axis=0, tiled=True
    )
    spots = jnp.arange(count, dtype=jnp.int32)
    margins = jnp.sum(
        jnp.where(place.reshape(vectors, 1) == spots[None, :], returned.reshape(1, count), 0.0),
        axis=1,
    )
    return fresh, margins


def solution(mesh):
    groups, members = mesh.devices.shape
    chip_mesh = Mesh(mesh.devices.reshape(groups // 2, 2, members), ("x", "core", "mem"))
    everywhere = ("x", "core", "mem")
    placed = (
        P(everywhere, None),
        P(everywhere),
        P(everywhere),
        P(),
        P(everywhere, None),
    )
    return jax.shard_map(
        on_device,
        mesh=chip_mesh,
        in_specs=placed,
        out_specs=(P(everywhere, None), P(everywhere)),
        check_vma=False,
    )
```

```python
import functools

import jax
import jax.numpy as jnp
from jax import lax
from jax.experimental import pallas as pl
from jax.experimental.pallas import tpu as pltpu
from jax.sharding import Mesh
from jax.sharding import PartitionSpec as P

F32 = jnp.float32
BF16 = jnp.bfloat16
LANES = 128
TILE = 8
NOTES = 16
CUT = 5
SMEM = pl.BlockSpec(memory_space=pltpu.SMEM)
VMEM = pl.BlockSpec(memory_space=pltpu.VMEM)


def rows_of(shape):
    return lax.broadcasted_iota(jnp.int32, shape, 0).astype(F32)


def lanes_of(shape):
    return lax.broadcasted_iota(jnp.int32, shape, 1).astype(F32)


def hot(condition):
    return jnp.where(condition, 1.0, 0.0).astype(BF16)


def dot(a, b, contract):
    return lax.dot_general(a, b, (contract, ((), ())), preferred_element_type=F32)


def whole(a, size):
    return jnp.floor((a + 0.5) * (1.0 / size))


def call(kernel, name, out_shape, flops, *args, scalars=None):
    specs = [VMEM] * len(args)
    if scalars is not None:
        specs = [SMEM] + specs
        args = (scalars,) + args
    return pl.pallas_call(
        kernel,
        in_specs=specs,
        out_shape=out_shape,
        compiler_params=pltpu.CompilerParams(vmem_limit_bytes=56 * 2**20),
        cost_estimate=pl.CostEstimate(flops=flops, bytes_accessed=2**21, transcendentals=0),
        name=name,
    )(*args)


def prepare(members, capacity, cut, first, second, table, embeddings, one, two, place):
    vectors = first.shape[1]
    slots = table[...]
    local = slots & (LANES - 1)
    owner = (slots // LANES) & (members - 1)
    group = slots // (LANES * members)
    planes = jnp.concatenate([local, owner, group], axis=1).astype(F32).astype(BF16)

    def look_up(ids):
        row = (ids // LANES).astype(F32)
        lane = (ids & (LANES - 1)).astype(F32)
        found = dot(planes, hot(rows_of((table.shape[0], vectors)) == row), ((0,), (0,)))
        mask = rows_of((LANES, vectors)) == lane

        def pick(k):
            return jnp.sum(
                jnp.where(mask, found[k * LANES : (k + 1) * LANES], 0.0), axis=0, keepdims=True
            )

        return pick(0), pick(1), pick(2)

    first_local, first_owner, first_group = look_up(first[...])
    second_local, _, second_group = look_up(second[...])
    is_owner = rows_of((members, vectors)) == first_owner
    before = hot(rows_of((vectors, vectors)) < lanes_of((vectors, vectors)))
    earlier = dot(hot(is_owner), before, ((1,), (0,)))
    rank = jnp.sum(jnp.where(is_owner, earlier, 0.0), axis=0, keepdims=True)
    place[...] = (first_owner * capacity + rank).astype(jnp.int32)
    spot = jnp.where(rank < TILE, first_owner * TILE + rank, rank * members + first_owner)
    order = hot(rows_of((members * capacity, vectors)) == spot)
    packed = dot(order, embeddings[...], ((1,), (0,)))
    ranked = rows_of((16, vectors)) == rank
    digits = [first_group + 1.0, first_local, second_group + 1.0, second_local]
    spread = [jnp.where(ranked, digit, 0.0) for digit in digits]
    spread.append(jnp.zeros((LANES - 16 * len(digits), vectors), F32))
    labels = dot(hot(is_owner), jnp.concatenate(spread, axis=0).astype(BF16), ((1,), (1,)))
    for out, start, stop, tail in (
        (one, 0, cut, [labels]),
        (two, cut, embeddings.shape[1] // LANES, []),
    ):
        pieces = [
            packed[: TILE * members, j * LANES : (j + 1) * LANES].reshape(members, TILE, LANES)
            for j in range(start, stop)
        ]
        rest = [
            packed[p * members : (p + 1) * members, j * LANES : (j + 1) * LANES]
            for p in range(TILE, capacity)
            for j in range(start, stop)
        ] + tail
        rest += [jnp.zeros((members, LANES), F32)] * (-len(rest) % TILE)
        for k in range(0, len(rest), TILE):
            pieces.append(jnp.stack(rest[k : k + TILE], axis=1))
        out[...] = jnp.concatenate(pieces, axis=1).astype(BF16)


def payload_rows(capacity, parts, labels):
    rows = capacity * parts + labels
    return rows + -rows % TILE


def unpack(capacity, labelled, arrived, box):
    members = arrived.shape[0]
    count = members * capacity
    parts = box.shape[1] // LANES
    values = arrived[...].astype(F32)
    for j in range(parts):
        at = slice(j * LANES, (j + 1) * LANES)
        box[: TILE * members, at] = (
            values[:, j * TILE : (j + 1) * TILE].reshape(TILE * members, LANES).astype(BF16)
        )
        for p in range(TILE, capacity):
            box[p * members : (p + 1) * members, at] = values[:, p * parts + j].astype(BF16)
    if not labelled:
        return
    labels = values[:, capacity * parts].astype(BF16)
    vector = lanes_of((members, count))
    from_member = jnp.where(
        vector < TILE * members, whole(vector, TILE), vector - members * whole(vector, members)
    )
    found = dot(labels, hot(rows_of((members, count)) == from_member), ((0,), (0,)))
    vector = lanes_of((16, count))
    rank = jnp.where(
        vector < TILE * members, vector - TILE * whole(vector, TILE), whole(vector, members)
    )
    ranked = rows_of((16, count)) == rank
    rows = [
        jnp.sum(jnp.where(ranked, found[k * 16 : (k + 1) * 16], 0.0), axis=0, keepdims=True)
        for k in range(4)
    ]
    notes = jnp.concatenate(rows + [jnp.zeros((NOTES - 4, count), F32)], axis=0)
    if count < box.shape[1]:
        notes = jnp.concatenate(
            [notes, jnp.zeros((NOTES, box.shape[1] - count), F32)], axis=1
        )
    box[count : count + NOTES] = notes.astype(BF16)


def index(chips, where, notes, k, ahead):
    group = notes[2 * k : 2 * k + 1] - 1.0
    local = notes[2 * k + 1 : 2 * k + 2]
    chip = whole(group, 2)
    core = group - 2.0 * chip
    if ahead:
        chip = chip - where[0].astype(F32)
        chip = jnp.where(chip < 0.0, chip + chips, chip)
    mine = (group >= 0.0) & (core == where[1].astype(F32))
    return jnp.where(mine, chip * LANES + local, -1.0)


def sums_one(chips, count, where, box, *refs):
    earlier, out = refs[:-1], refs[-1]
    width = box.shape[1]
    notes = box[count : count + NOTES, :count].astype(F32)
    at = index(chips, where, notes, 0, False)
    ones = jnp.ones((NOTES, count), BF16)
    for pair in range(0, chips, 2):
        table = hot(rows_of((2 * LANES, count)) + pair * LANES == at)
        total = dot(table, box[0:count, :], ((1,), (0,)))
        hits = dot(ones, table, ((1,), (1,)))
        high = whole(hits, 256)
        left = hits - 256.0 * high
        middle = whole(left, 16)
        low = left - 16.0 * middle
        for n in range(2):
            half = slice(n * LANES, (n + 1) * LANES)
            digits = [low[:, half], middle[:, half], high[:, half]]
            digits.append(jnp.zeros((NOTES, width - 3 * LANES), F32))
            block = jnp.concatenate([total[half], jnp.concatenate(digits, axis=1)], axis=0)
            to = slice((pair + n) * (LANES + NOTES), (pair + n + 1) * (LANES + NOTES))
            if earlier:
                block = block + earlier[0][to].astype(F32)
            out[to] = block.astype(BF16)


def sums_two(chips, count, where, box, notes_box, *refs):
    earlier, outs = refs[: len(refs) - chips - 1], refs[len(refs) - chips - 1 :]
    notes = notes_box[count : count + NOTES, :count].astype(F32)
    at = index(chips, where, notes, 0, True)
    cut = outs[chips // 2].shape[1]
    for pair in range(0, chips, 2):
        table = hot(rows_of((2 * LANES, count)) + pair * LANES == at)
        total = dot(table, box[...], ((1,), (0,)))
        for n in range(2):
            block = total[n * LANES : (n + 1) * LANES]
            places = [(pair + n, block)]
            if pair + n == chips // 2:
                places = [(pair + n, block[:, :cut]), (chips, block[:, cut:])]
            for place, value in places:
                if earlier:
                    value = value + earlier[place][...].astype(F32)
                outs[place][...] = value.astype(BF16)


def counts_of(digits):
    identity = hot(rows_of((LANES, LANES)) == lanes_of((LANES, LANES)))

    def column(k):
        return dot(identity, digits[:, k * LANES : (k + 1) * LANES], ((1,), (1,)))[:, 0:1]

    return column(0) + 16.0 * column(1) + 256.0 * column(2)


def refit_one(summed, old, fresh):
    width = summed.shape[1]
    counts = counts_of(summed[LANES : LANES + NOTES])
    total = summed[0:LANES].astype(F32) + old[:, :width].astype(F32)
    fresh[...] = (total / (counts + 1.0)).astype(BF16)


def refit_two(summed, fresh_one, mine, above, below, old, fresh_two, fresh):
    width = summed.shape[1]
    counts = counts_of(summed[LANES : LANES + NOTES])
    total = mine[...].astype(F32) + above[...].astype(F32) + below[...].astype(F32)
    total = total + old[:, width:].astype(F32)
    part = (total / (counts + 1.0)).astype(BF16)
    fresh_two[...] = part
    fresh[:, :width] = fresh_one[...]
    fresh[:, width:] = part


def score(chips, count, ahead, places, where, notes_own, notes_other, own, other, *refs):
    blocks, out = refs[: len(places)], refs[-1]
    before = refs[len(places) : -1]
    lists = 2 * LANES
    items = []
    for start, block in zip(places, blocks):
        rows = block.shape[0]
        items += [(start + r, block, r) for r in range(0, rows, LANES)]
    totals = [jnp.zeros((1, count), F32)] * 2
    for k in range(0, len(items), 2):
        pair = items[k : k + 2]
        values = jnp.concatenate([block[r : r + LANES] for _, block, r in pair], axis=0)
        size = jnp.sum(values.astype(F32) ** 2, axis=1, keepdims=True)
        lists = LANES * len(pair)
        row = rows_of((lists, count))
        if len(pair) == 2:
            row = jnp.where(row < LANES, row + pair[0][0], row + (pair[1][0] - LANES))
        else:
            row = row + pair[0][0]
        for n, (notes_box, box) in enumerate(((notes_own, own), (notes_other, other))):
            notes = notes_box[count : count + NOTES, :count].astype(F32)
            distance = size - 2.0 * dot(values, box[0:count, :], ((1,), (1,)))
            is_first = row == index(chips, where, notes, 0, ahead)
            is_second = row == index(chips, where, notes, 1, ahead)
            totals[n] = totals[n] + jnp.sum(
                jnp.where(is_second, distance, 0.0) - jnp.where(is_first, distance, 0.0),
                axis=0,
                keepdims=True,
            )
    total = jnp.concatenate(totals, axis=0)
    for earlier in before:
        total = total + earlier[...]
    out[...] = total


def shifted(axis, size, step):
    pairs = [(i, (i + step) % size) for i in range(size)]
    return lambda a: lax.ppermute(a, axis, pairs)


def add(a, b):
    return (a.astype(F32) + b.astype(F32)).astype(BF16)


def ring_sum(up, down, blocks):
    cut = blocks[4].shape[1]
    above = up(blocks[4])
    below = down(blocks[8])
    above = up(jnp.concatenate([add(blocks[3][:, :cut], above), blocks[3][:, cut:]], axis=1))
    below = down(jnp.concatenate([blocks[5][:, :cut], add(blocks[5][:, cut:], below)], axis=1))
    above = up(add(blocks[2], above))
    below = down(add(blocks[6], below))
    above = up(add(blocks[1], above))
    below = down(add(blocks[7], below))
    return blocks[0], above, below


def ring_gather(up, down, cut, block):
    above, below = [block], [block]
    for _ in range(3):
        above.append(up(above[-1]))
        below.append(down(below[-1]))
    far = jnp.concatenate([up(above[3][:, :cut]), down(below[3][:, cut:])], axis=1)
    return [block, below[1], below[2], below[3], far, above[3], above[2], above[1]]


def on_device(embeddings, assignment, second_choice, list_slot, old_centroids):
    vectors, width = embeddings.shape
    lists = old_centroids.shape[0]
    members = lax.axis_size("mem")
    chips = lax.axis_size("x")
    capacity = vectors // members + 2
    count = members * capacity
    parts = width // LANES
    cut = CUT
    wide, narrow = cut * LANES, width - cut * LANES
    up = shifted("x", chips, 1)
    down = shifted("x", chips, -1)
    across = shifted("core", 2, 1)

    def shape(*dims, kind=BF16):
        return jax.ShapeDtypeStruct(dims, kind)

    def exchange(a):
        return lax.all_to_all(a, "mem", split_axis=0, concat_axis=0, tiled=True)

    where = jnp.stack([lax.axis_index("x"), lax.axis_index("core")]).astype(jnp.int32)
    sent_one, sent_two, place = call(
        functools.partial(prepare, members, capacity, cut),
        "prepare",
        (
            shape(members, payload_rows(capacity, cut, 1), LANES),
            shape(members, payload_rows(capacity, parts - cut, 0), LANES),
            shape(1, vectors, kind=jnp.int32),
        ),
        2**31,
        assignment.reshape(1, vectors),
        second_choice.reshape(1, vectors),
        list_slot.reshape(-1, LANES),
        embeddings,
    )
    arrived_one = exchange(sent_one)
    arrived_two = exchange(sent_two)

    own = call(
        functools.partial(unpack, capacity, True),
        "unpack",
        shape(count + NOTES, wide),
        2**24,
        arrived_one,
    )
    other = across(own)
    kernel = functools.partial(sums_one, chips, count)
    block = shape(chips * (lists + NOTES), wide)
    sums = call(kernel, "sums_one", block, 2**31, own, scalars=where)
    sums = call(kernel, "sums_one", block, 2**31, other, sums, scalars=where)
    summed = lax.psum_scatter(sums, "x", scatter_dimension=0, tiled=True)

    own_two = call(
        functools.partial(unpack, capacity, False), "unpack", shape(count, narrow), 2**24, arrived_two
    )
    other_two = across(own_two)
    kernel = functools.partial(sums_two, chips, count)
    far = (narrow // LANES + 1) // 2 * LANES
    outs = [shape(lists, far if k == chips // 2 else narrow) for k in range(chips)]
    outs.append(shape(lists, narrow - far))
    blocks = call(kernel, "sums_two", outs, 2**31, own_two, own, scalars=where)
    blocks = call(kernel, "sums_two", outs, 2**31, other_two, other, *blocks, scalars=where)
    mine, above, below = ring_sum(up, down, blocks)

    fresh_one = call(refit_one, "refit", shape(lists, wide), 2**24, summed, old_centroids)
    all_one = lax.all_gather(fresh_one, "x", axis=0, tiled=True)
    fresh_two, fresh = call(
        refit_two,
        "refit",
        (shape(lists, narrow), shape(lists, width)),
        2**24,
        summed,
        fresh_one,
        mine,
        above,
        below,
        old_centroids,
    )
    gathered = ring_gather(up, down, far, fresh_two)

    def scored(ahead, places, a, b, *rest):
        return call(
            functools.partial(score, chips, count, ahead, places),
            "score",
            shape(2, count, kind=F32),
            2**31,
            own,
            other,
            a,
            b,
            *rest,
            scalars=where,
        )

    near = [0, 1, 7, 2, 6]
    last = [3, 5, 4]
    total = scored(
        True, [k * LANES for k in near], own_two, other_two, *[gathered[k] for k in near]
    )
    total = scored(False, [0], own, other, all_one, total)
    total = scored(
        True, [k * LANES for k in last], own_two, other_two, *[gathered[k] for k in last], total
    )
    margin = (total[0] + across(total[1])) * (1.0 / width)
    margin = jnp.concatenate(
        [
            margin[: TILE * members].reshape(members, TILE),
            margin[TILE * members :].reshape(capacity - TILE, members).T,
        ],
        axis=1,
    )
    returned = exchange(margin.reshape(members, 1, capacity))
    spots = jnp.arange(count, dtype=jnp.int32)
    margins = jnp.sum(
        jnp.where(place.reshape(vectors, 1) == spots[None, :], returned.reshape(1, count), 0.0),
        axis=1,
    )
    return fresh, margins


def solution(mesh):
    groups, members = mesh.devices.shape
    chip_mesh = Mesh(mesh.devices.reshape(groups // 2, 2, members), ("x", "core", "mem"))
    everywhere = ("x", "core", "mem")
    placed = (
        P(everywhere, None),
        P(everywhere),
        P(everywhere),
        P(),
        P(everywhere, None),
    )
    return jax.shard_map(
        on_device,
        mesh=chip_mesh,
        in_specs=placed,
        out_specs=(P(everywhere, None), P(everywhere)),
        check_vma=False,
    )
```

```python
import functools

import jax
import jax.numpy as jnp
from jax import lax
from jax.experimental import pallas as pl
from jax.experimental.pallas import tpu as pltpu
from jax.sharding import Mesh
from jax.sharding import PartitionSpec as P

F32 = jnp.float32
BF16 = jnp.bfloat16
LANES = 128
TILE = 8
NOTES = 16
LIMIT = 40 * 2**20
SMEM = pl.BlockSpec(memory_space=pltpu.SMEM)
VMEM = pl.BlockSpec(memory_space=pltpu.VMEM)


def rows_of(shape):
    return lax.broadcasted_iota(jnp.int32, shape, 0).astype(F32)


def lanes_of(shape):
    return lax.broadcasted_iota(jnp.int32, shape, 1).astype(F32)


def hot(condition):
    return jnp.where(condition, 1.0, 0.0).astype(BF16)


def dot(a, b, contract):
    return lax.dot_general(a, b, (contract, ((), ())), preferred_element_type=F32)


def whole(a, size):
    return jnp.floor((a + 0.5) * (1.0 / size))


def call(kernel, name, out_shape, flops, *args, scalars=None):
    specs = [VMEM] * len(args)
    if scalars is not None:
        specs = [SMEM] + specs
        args = (scalars,) + args
    return pl.pallas_call(
        kernel,
        in_specs=specs,
        out_shape=out_shape,
        compiler_params=pltpu.CompilerParams(vmem_limit_bytes=LIMIT),
        cost_estimate=pl.CostEstimate(flops=flops, bytes_accessed=2**21, transcendentals=0),
        name=name,
    )(*args)


def prepare(members, capacity, first, second, table, embeddings, payload, place):
    vectors = first.shape[1]
    parts = embeddings.shape[1] // LANES
    slots = table[...]
    local = slots & (LANES - 1)
    owner = (slots // LANES) & (members - 1)
    group = slots // (LANES * members)
    planes = jnp.concatenate([local, owner, group], axis=1).astype(F32).astype(BF16)

    def look_up(ids):
        row = (ids // LANES).astype(F32)
        lane = (ids & (LANES - 1)).astype(F32)
        found = dot(planes, hot(rows_of((table.shape[0], vectors)) == row), ((0,), (0,)))
        mask = rows_of((LANES, vectors)) == lane

        def pick(k):
            return jnp.sum(
                jnp.where(mask, found[k * LANES : (k + 1) * LANES], 0.0), axis=0, keepdims=True
            )

        return pick(0), pick(1), pick(2)

    first_local, first_owner, first_group = look_up(first[...])
    second_local, _, second_group = look_up(second[...])
    is_owner = rows_of((members, vectors)) == first_owner
    before = hot(rows_of((vectors, vectors)) < lanes_of((vectors, vectors)))
    earlier = dot(hot(is_owner), before, ((1,), (0,)))
    rank = jnp.sum(jnp.where(is_owner, earlier, 0.0), axis=0, keepdims=True)
    place[...] = (first_owner * capacity + rank).astype(jnp.int32)
    spot = jnp.where(rank < TILE, first_owner * TILE + rank, rank * members + first_owner)
    order = hot(rows_of((members * capacity, vectors)) == spot)
    packed = dot(order, embeddings[...], ((1,), (0,)))
    ranked = rows_of((16, vectors)) == rank
    digits = [first_group + 1.0, first_local, second_group + 1.0, second_local]
    spread = [jnp.where(ranked, digit, 0.0) for digit in digits]
    spread.append(jnp.zeros((LANES - 16 * len(digits), vectors), F32))
    labels = dot(hot(is_owner), jnp.concatenate(spread, axis=0).astype(BF16), ((1,), (1,)))
    pieces = [
        packed[: TILE * members, j * LANES : (j + 1) * LANES].reshape(members, TILE, LANES)
        for j in range(parts)
    ]
    rest = [
        packed[p * members : (p + 1) * members, j * LANES : (j + 1) * LANES]
        for p in range(TILE, capacity)
        for j in range(parts)
    ]
    for k in range(0, len(rest), TILE):
        pieces.append(jnp.stack(rest[k : k + TILE], axis=1))
    pieces.append(jnp.broadcast_to(labels[:, None, :], (members, TILE, LANES)))
    payload[...] = jnp.concatenate(pieces, axis=1).astype(BF16)


def unpack(capacity, arrived, box):
    members = arrived.shape[0]
    count = members * capacity
    parts = box.shape[1] // LANES
    values = arrived[...].astype(F32)
    for j in range(parts):
        at = slice(j * LANES, (j + 1) * LANES)
        box[: TILE * members, at] = (
            values[:, j * TILE : (j + 1) * TILE].reshape(TILE * members, LANES).astype(BF16)
        )
        for p in range(TILE, capacity):
            box[p * members : (p + 1) * members, at] = values[:, p * parts + j].astype(BF16)
    labels = values[:, capacity * parts].astype(BF16)
    vector = lanes_of((members, count))
    from_member = jnp.where(
        vector < TILE * members, whole(vector, TILE), vector - members * whole(vector, members)
    )
    found = dot(labels, hot(rows_of((members, count)) == from_member), ((0,), (0,)))
    vector = lanes_of((16, count))
    rank = jnp.where(
        vector < TILE * members, vector - TILE * whole(vector, TILE), whole(vector, members)
    )
    ranked = rows_of((16, count)) == rank
    rows = [
        jnp.sum(jnp.where(ranked, found[k * 16 : (k + 1) * 16], 0.0), axis=0, keepdims=True)
        for k in range(4)
    ]
    notes = jnp.concatenate(rows + [jnp.zeros((NOTES - 4, count), F32)], axis=0)
    if count < box.shape[1]:
        notes = jnp.concatenate(
            [notes, jnp.zeros((NOTES, box.shape[1] - count), F32)], axis=1
        )
    box[count : count + NOTES] = notes.astype(BF16)


def index(chips, where, notes, k):
    group = notes[2 * k : 2 * k + 1] - 1.0
    local = notes[2 * k + 1 : 2 * k + 2]
    chip = whole(group, 2)
    core = group - 2.0 * chip
    own_core = where[1].astype(F32)
    ahead = (chip - where[0].astype(F32)) * (1.0 - 2.0 * own_core)
    ahead = jnp.where(ahead < 0.0, ahead + chips, ahead)
    mine = (group >= 0.0) & (core == own_core)
    return jnp.where(mine, ahead * LANES + local, -1.0)


def sums(chips, count, where, box, *refs):
    earlier, outs = refs[: len(refs) - chips - 1], refs[len(refs) - chips - 1 :]
    width = box.shape[1]
    notes = box[count : count + NOTES, :count].astype(F32)
    table = hot(rows_of((chips * LANES, count)) == index(chips, where, notes, 0))
    total = dot(table, box[0:count, :], ((1,), (0,)))
    hits = dot(jnp.ones((NOTES, count), BF16), table, ((1,), (1,)))
    high = whole(hits, 256)
    left = hits - 256.0 * high
    middle = whole(left, 16)
    low = left - 16.0 * middle
    cut = width // 2
    for k in range(chips):
        at = slice(k * LANES, (k + 1) * LANES)
        digits = [low[:, at], middle[:, at], high[:, at]]
        digits.append(jnp.zeros((NOTES, width - 3 * LANES), F32))
        block = jnp.concatenate([total[at], jnp.concatenate(digits, axis=1)], axis=0)
        places = [(k, block)]
        if k == chips // 2:
            places = [(k, block[:, :cut]), (chips, block[:, cut:])]
        for place, value in places:
            if earlier:
                value = value + earlier[place][...].astype(F32)
            outs[place][...] = value.astype(BF16)


def counts_of(digits):
    identity = hot(rows_of((LANES, LANES)) == lanes_of((LANES, LANES)))

    def column(k):
        return dot(identity, digits[:, k * LANES : (k + 1) * LANES], ((1,), (1,)))[:, 0:1]

    return column(0) + 16.0 * column(1) + 256.0 * column(2)


def refit(mine, above, below, old, fresh):
    counts = counts_of(
        add(add(mine[LANES:], above[LANES:]), below[LANES:])
    )
    total = mine[:LANES].astype(F32) + above[:LANES].astype(F32) + below[:LANES].astype(F32)
    fresh[...] = ((total + old[...].astype(F32)) / (counts + 1.0)).astype(BF16)


def score(chips, count, places, where, own, other, *refs):
    blocks, out = refs[: len(places)], refs[-1]
    before = refs[len(places) : -1]
    values = jnp.concatenate([block[...] for block in blocks], axis=0)
    size = jnp.sum(values.astype(F32) ** 2, axis=1, keepdims=True)
    row = jnp.concatenate([rows_of((LANES, count)) + place for place in places], axis=0)
    totals = []
    for box in (own, other):
        notes = box[count : count + NOTES, :count].astype(F32)
        distance = size - 2.0 * dot(values, box[0:count, :], ((1,), (1,)))
        is_first = row == index(chips, where, notes, 0)
        is_second = row == index(chips, where, notes, 1)
        totals.append(
            jnp.sum(
                jnp.where(is_second, distance, 0.0) - jnp.where(is_first, distance, 0.0),
                axis=0,
                keepdims=True,
            )
        )
    total = jnp.concatenate(totals, axis=0)
    for earlier in before:
        total = total + earlier[...]
    out[...] = total


def add(a, b):
    return (a.astype(F32) + b.astype(F32)).astype(BF16)


def ring_sum(up, down, blocks):
    cut = blocks[4].shape[1]
    above = up(blocks[4])
    below = down(blocks[8])
    above = up(jnp.concatenate([add(blocks[3][:, :cut], above), blocks[3][:, cut:]], axis=1))
    below = down(jnp.concatenate([blocks[5][:, :cut], add(blocks[5][:, cut:], below)], axis=1))
    above = up(add(blocks[2], above))
    below = down(add(blocks[6], below))
    above = up(add(blocks[1], above))
    below = down(add(blocks[7], below))
    return blocks[0], above, below


def ring_gather(up, down, cut, block):
    above, below = [block], [block]
    for _ in range(3):
        above.append(up(above[-1]))
        below.append(down(below[-1]))
    far = jnp.concatenate([up(above[3][:, :cut]), down(below[3][:, cut:])], axis=1)
    return [block, below[1], below[2], below[3], far, above[3], above[2], above[1]]


def on_device(embeddings, assignment, second_choice, list_slot, old_centroids):
    vectors, width = embeddings.shape
    lists = old_centroids.shape[0]
    members = lax.axis_size("mem")
    chips = lax.axis_size("x")
    capacity = vectors // members + 2
    count = members * capacity
    half = width // 2

    def along(step):
        pairs = [(2 * i, 2 * ((i + step) % chips)) for i in range(chips)]
        pairs += [(2 * i + 1, 2 * ((i - step) % chips) + 1) for i in range(chips)]
        return lambda a: lax.ppermute(a, ("x", "core"), pairs)

    up, down = along(1), along(-1)

    def across(a):
        return lax.ppermute(a, "core", [(0, 1), (1, 0)])

    def shape(*dims, kind=BF16):
        return jax.ShapeDtypeStruct(dims, kind)

    def exchange(a):
        return lax.all_to_all(a, "mem", split_axis=0, concat_axis=0, tiled=True)

    where = jnp.stack([lax.axis_index("x"), lax.axis_index("core")]).astype(jnp.int32)
    payload, place = call(
        functools.partial(prepare, members, capacity),
        "prepare",
        (
            shape(members, capacity * width // LANES + TILE, LANES),
            shape(1, vectors, kind=jnp.int32),
        ),
        2**31,
        assignment.reshape(1, vectors),
        second_choice.reshape(1, vectors),
        list_slot.reshape(-1, LANES),
        embeddings,
    )
    arrived = exchange(payload)
    own = call(
        functools.partial(unpack, capacity), "unpack", shape(count + NOTES, width), 2**24, arrived
    )
    other = across(own)
    kernel = functools.partial(sums, chips, count)
    outs = [shape(lists + NOTES, half if k == chips // 2 else width) for k in range(chips)]
    outs.append(shape(lists + NOTES, half))
    blocks = call(kernel, "sums", outs, 2**31, own, scalars=where)
    blocks = call(kernel, "sums", outs, 2**31, other, *blocks, scalars=where)
    fresh = call(
        refit, "refit", shape(lists, width), 2**24, *ring_sum(up, down, blocks), old_centroids
    )
    gathered = ring_gather(up, down, half, fresh)

    def scored(near, *rest):
        return call(
            functools.partial(score, chips, count, [k * LANES for k in near]),
            "score",
            shape(2, count, kind=F32),
            2**31,
            own,
            other,
            *[gathered[k] for k in near],
            *rest,
            scalars=where,
        )

    total = scored([0, 1, 7, 2, 6])
    total = scored([3, 5, 4], total)
    margin = (total[0] + across(total[1])) * (1.0 / width)
    margin = jnp.concatenate(
        [
            margin[: TILE * members].reshape(members, TILE),
            margin[TILE * members :].reshape(capacity - TILE, members).T,
        ],
        axis=1,
    )
    returned = exchange(margin.reshape(members, 1, capacity))
    spots = jnp.arange(count, dtype=jnp.int32)
    margins = jnp.sum(
        jnp.where(place.reshape(vectors, 1) == spots[None, :], returned.reshape(1, count), 0.0),
        axis=1,
    )
    return fresh, margins


def solution(mesh):
    groups, members = mesh.devices.shape
    chip_mesh = Mesh(mesh.devices.reshape(groups // 2, 2, members), ("x", "core", "mem"))
    everywhere = ("x", "core", "mem")
    placed = (
        P(everywhere, None),
        P(everywhere),
        P(everywhere),
        P(),
        P(everywhere, None),
    )
    return jax.shard_map(
        on_device,
        mesh=chip_mesh,
        in_specs=placed,
        out_specs=(P(everywhere, None), P(everywhere)),
        check_vma=False,
    )
```

```python
import functools

import jax
import jax.numpy as jnp
from jax import lax
from jax.experimental import pallas as pl
from jax.experimental.pallas import tpu as pltpu
from jax.sharding import Mesh
from jax.sharding import PartitionSpec as P

F32 = jnp.float32
BF16 = jnp.bfloat16
LANES = 128
TILE = 8
NOTES = 32
LIMIT = 40 * 2**20
SMEM = pl.BlockSpec(memory_space=pltpu.SMEM)
VMEM = pl.BlockSpec(memory_space=pltpu.VMEM)


def rows_of(shape):
    return lax.broadcasted_iota(jnp.int32, shape, 0).astype(F32)


def lanes_of(shape):
    return lax.broadcasted_iota(jnp.int32, shape, 1).astype(F32)


def hot(condition):
    return jnp.where(condition, 1.0, 0.0).astype(BF16)


def dot(a, b, contract):
    return lax.dot_general(a, b, (contract, ((), ())), preferred_element_type=F32)


def whole(a, size):
    return jnp.floor((a + 0.5) * (1.0 / size))


def call(kernel, name, out_shape, flops, *args, scalars=None, scratch=()):
    specs = [VMEM] * len(args)
    if scalars is not None:
        specs = [SMEM] + specs
        args = (scalars,) + args
    return pl.pallas_call(
        kernel,
        in_specs=specs,
        out_shape=out_shape,
        scratch_shapes=scratch,
        compiler_params=pltpu.CompilerParams(vmem_limit_bytes=LIMIT),
        cost_estimate=pl.CostEstimate(flops=flops, bytes_accessed=2**21, transcendentals=0),
        name=name,
    )(*args)


def prepare(members, capacity, first, second, table, embeddings, payload, place):
    vectors = first.shape[1]
    parts = embeddings.shape[1] // LANES
    slots = table[...]
    local = slots & (LANES - 1)
    owner = (slots // LANES) & (members - 1)
    group = slots // (LANES * members)
    planes = jnp.concatenate([local, owner, group], axis=1).astype(F32).astype(BF16)

    def look_up(ids):
        row = (ids // LANES).astype(F32)
        lane = (ids & (LANES - 1)).astype(F32)
        found = dot(planes, hot(rows_of((table.shape[0], vectors)) == row), ((0,), (0,)))
        mask = rows_of((LANES, vectors)) == lane

        def pick(k):
            return jnp.sum(
                jnp.where(mask, found[k * LANES : (k + 1) * LANES], 0.0), axis=0, keepdims=True
            )

        return pick(0), pick(1), pick(2)

    first_local, first_owner, first_group = look_up(first[...])
    second_local, _, second_group = look_up(second[...])
    is_owner = rows_of((members, vectors)) == first_owner
    before = hot(rows_of((vectors, vectors)) < lanes_of((vectors, vectors)))
    earlier = dot(hot(is_owner), before, ((1,), (0,)))
    rank = jnp.sum(jnp.where(is_owner, earlier, 0.0), axis=0, keepdims=True)
    place[...] = (first_owner * capacity + rank).astype(jnp.int32)
    spot = jnp.where(rank < TILE, first_owner * TILE + rank, rank * members + first_owner)
    order = hot(rows_of((members * capacity, vectors)) == spot)
    packed = dot(order, embeddings[...], ((1,), (0,)))
    ranked = rows_of((16, vectors)) == rank
    digits = [first_group + 1.0, first_local, second_group + 1.0, second_local]
    spread = [jnp.where(ranked, digit, 0.0) for digit in digits]
    spread.append(jnp.zeros((LANES - 16 * len(digits), vectors), F32))
    labels = dot(hot(is_owner), jnp.concatenate(spread, axis=0).astype(BF16), ((1,), (1,)))
    pieces = [
        packed[: TILE * members, j * LANES : (j + 1) * LANES].reshape(members, TILE, LANES)
        for j in range(parts)
    ]
    rest = [
        packed[p * members : (p + 1) * members, j * LANES : (j + 1) * LANES]
        for p in range(TILE, capacity)
        for j in range(parts)
    ]
    for k in range(0, len(rest), TILE):
        pieces.append(jnp.stack(rest[k : k + TILE], axis=1))
    pieces.append(jnp.broadcast_to(labels[:, None, :], (members, TILE, LANES)))
    payload[...] = jnp.concatenate(pieces, axis=1).astype(BF16)


def spread(capacity, arrived, old, out):
    members = arrived.shape[0]
    count = members * capacity
    chips, rows, _ = out.shape
    slots = rows - NOTES - LANES
    values = arrived[...].astype(F32)
    labels = values[:, capacity * chips].astype(BF16)
    vector = lanes_of((members, slots))
    from_member = jnp.where(
        vector < TILE * members, whole(vector, TILE), vector - members * whole(vector, members)
    )
    found = dot(labels, hot(rows_of((members, slots)) == from_member), ((0,), (0,)))
    vector = lanes_of((16, slots))
    rank = jnp.where(
        vector < TILE * members, vector - TILE * whole(vector, TILE), whole(vector, members)
    )
    ranked = rows_of((16, slots)) == rank
    notes = []
    for k in range(4):
        row = jnp.sum(jnp.where(ranked, found[k * 16 : (k + 1) * 16], 0.0), axis=0, keepdims=True)
        notes += [row[:, q : q + LANES] for q in range(0, slots, LANES)]
    notes.append(jnp.zeros((NOTES - len(notes), LANES), F32))
    notes = jnp.concatenate(notes, axis=0).astype(BF16)
    for j in range(chips):
        out[j, : TILE * members] = (
            values[:, j * TILE : (j + 1) * TILE].reshape(TILE * members, LANES).astype(BF16)
        )
        for p in range(TILE, capacity):
            out[j, p * members : (p + 1) * members] = values[:, p * chips + j].astype(BF16)
        if slots > count:
            out[j, count:slots] = jnp.zeros((slots - count, LANES), BF16)
        out[j, slots : slots + NOTES] = notes
        out[j, slots + NOTES :] = old[:, j * LANES : (j + 1) * LANES]


def labels_of(slots, notes, k):
    chunks = slots // LANES

    def row(d):
        return jnp.concatenate(
            [notes[d * chunks + q : d * chunks + q + 1] for q in range(chunks)], axis=1
        )

    return row(2 * k) - 1.0, row(2 * k + 1)


def sums(groups, where, columns, out, total):
    chips, rows, _ = columns.shape
    slots = rows - NOTES - LANES
    total[...] = jnp.zeros(total.shape, F32)

    def step(s, _):
        notes = columns[s, slots : slots + NOTES].astype(F32)
        group, local = labels_of(slots, notes, 0)
        at = hot(rows_of((LANES, slots)) == local)
        table = jnp.concatenate([at * hot(group == float(g)) for g in range(groups)], axis=0)
        vectors = jnp.concatenate(
            [columns[s, 0:slots], jnp.ones((slots, LANES), BF16)], axis=1
        )
        total[...] += dot(table, vectors, ((1,), (0,)))
        return 0

    lax.fori_loop(0, chips, step, 0)
    identity = rows_of((LANES, LANES)) == lanes_of((LANES, LANES))
    counts = []
    for g in range(groups):
        at = slice(g * LANES, (g + 1) * LANES)
        old = columns[g // 2, slots + NOTES :].astype(F32)
        old = jnp.where(where[1] == g % 2, old, 0.0)
        out[at] = (total[at, :LANES] + old).astype(BF16)
        counts.append(
            jnp.sum(jnp.where(identity, total[at, LANES:], 0.0), axis=0, keepdims=True)
        )
    counts = jnp.concatenate(counts, axis=0)
    high = whole(counts, 256)
    out[groups * LANES : groups * (LANES + 1)] = (counts - 256.0 * high).astype(BF16)
    out[groups * (LANES + 1) :] = high.astype(BF16)


def refit(groups, where, columns, mine, theirs, parts, margins, fresh):
    chips, rows, _ = columns.shape
    slots = rows - NOTES - LANES
    lists = groups * LANES

    def counts_of(sums):
        low = sums[lists : lists + groups].astype(F32)
        return low + 256.0 * sums[lists + groups :].astype(F32)

    counts = counts_of(mine) + counts_of(theirs) + 1.0
    identity = rows_of((LANES, LANES)) == lanes_of((LANES, LANES))
    sizes = []
    for g in range(groups):
        at = slice(g * LANES, (g + 1) * LANES)
        divisor = jnp.sum(jnp.where(identity, counts[g : g + 1], 0.0), axis=1, keepdims=True)
        total = mine[at].astype(F32) + theirs[at].astype(F32)
        value = (total / divisor).astype(BF16)
        fresh[at] = value
        sizes.append(jnp.sum(value.astype(F32) ** 2, axis=1, keepdims=True))
    for s in range(chips):
        one = fresh[2 * s * LANES : (2 * s + 1) * LANES]
        two = fresh[(2 * s + 1) * LANES : (2 * s + 2) * LANES]
        parts[s] = jnp.where(where[1] == 0, one.astype(F32), two.astype(F32)).astype(BF16)

    def step(s, _):
        notes = columns[s, slots : slots + NOTES].astype(F32)
        product = dot(fresh[...], columns[s, 0:slots], ((1,), (1,)))
        distances = [
            sizes[g] - 2.0 * product[g * LANES : (g + 1) * LANES] for g in range(groups)
        ]

        def pick(k):
            group, local = labels_of(slots, notes, k)
            found = jnp.zeros((LANES, slots), F32)
            for g in range(groups):
                found = jnp.where(group == float(g), distances[g], found)
            return jnp.where(rows_of((LANES, slots)) == local, found, 0.0)

        margins[pl.ds(s, 1), :] = jnp.sum(pick(1) - pick(0), axis=0, keepdims=True)
        return 0

    lax.fori_loop(0, chips, step, 0)


def on_device(embeddings, assignment, second_choice, list_slot, old_centroids):
    vectors, width = embeddings.shape
    lists = old_centroids.shape[0]
    members = lax.axis_size("mem")
    chips = lax.axis_size("x")
    capacity = vectors // members + 2
    count = members * capacity

    groups = 2 * chips
    slots = count + -count % LANES

    def across(a):
        return lax.ppermute(a, "core", [(0, 1), (1, 0)])

    def shape(*dims, kind=BF16):
        return jax.ShapeDtypeStruct(dims, kind)

    def exchange(axis, a):
        return lax.all_to_all(a, axis, split_axis=0, concat_axis=0, tiled=True)

    where = jnp.stack([lax.axis_index("x"), lax.axis_index("core")]).astype(jnp.int32)
    payload, place = call(
        functools.partial(prepare, members, capacity),
        "prepare",
        (
            shape(members, capacity * width // LANES + TILE, LANES),
            shape(1, vectors, kind=jnp.int32),
        ),
        2**31,
        assignment.reshape(1, vectors),
        second_choice.reshape(1, vectors),
        list_slot.reshape(-1, LANES),
        embeddings,
    )
    arrived = exchange("mem", payload)
    sent = call(
        functools.partial(spread, capacity),
        "spread",
        shape(chips, slots + NOTES + LANES, LANES),
        2**24,
        arrived,
        old_centroids,
    )
    columns = exchange("x", sent)
    mine = call(
        functools.partial(sums, groups),
        "sums",
        shape(groups * (LANES + 2), LANES),
        2**32,
        columns,
        scalars=where,
        scratch=[pltpu.VMEM((groups * LANES, 2 * LANES), F32)],
    )
    parts, scores = call(
        functools.partial(refit, groups),
        "refit",
        (shape(chips, lists, LANES), shape(chips, slots, kind=F32)),
        2**32,
        columns,
        mine,
        across(mine),
        scalars=where,
        scratch=[pltpu.VMEM((groups * LANES, LANES), BF16)],
    )
    scores = exchange("x", scores.reshape(chips, 1, slots))
    margin = jnp.sum(scores.reshape(chips, slots), axis=0) * (1.0 / width)
    fresh = exchange("x", parts).swapaxes(0, 1).reshape(lists, width)
    margin = jnp.concatenate(
        [
            margin[: TILE * members].reshape(members, TILE),
            margin[TILE * members : count].reshape(capacity - TILE, members).T,
        ],
        axis=1,
    )
    returned = exchange("mem", margin.reshape(members, 1, capacity))
    spots = jnp.arange(count, dtype=jnp.int32)
    margins = jnp.sum(
        jnp.where(place.reshape(vectors, 1) == spots[None, :], returned.reshape(1, count), 0.0),
        axis=1,
    )
    return fresh, margins


def solution(mesh):
    groups, members = mesh.devices.shape
    chip_mesh = Mesh(mesh.devices.reshape(groups // 2, 2, members), ("x", "core", "mem"))
    everywhere = ("x", "core", "mem")
    placed = (
        P(everywhere, None),
        P(everywhere),
        P(everywhere),
        P(),
        P(everywhere, None),
    )
    return jax.shard_map(
        on_device,
        mesh=chip_mesh,
        in_specs=placed,
        out_specs=(P(everywhere, None), P(everywhere)),
        check_vma=False,
    )
```

```python
import functools

import jax
import jax.numpy as jnp
from jax import lax
from jax.experimental import pallas as pl
from jax.experimental.pallas import tpu as pltpu
from jax.sharding import Mesh
from jax.sharding import PartitionSpec as P

F32 = jnp.float32
BF16 = jnp.bfloat16
LANES = 128
TILE = 8
NOTES = 32
LIMIT = 40 * 2**20
SMEM = pl.BlockSpec(memory_space=pltpu.SMEM)
VMEM = pl.BlockSpec(memory_space=pltpu.VMEM)


def rows_of(shape):
    return lax.broadcasted_iota(jnp.int32, shape, 0).astype(F32)


def lanes_of(shape):
    return lax.broadcasted_iota(jnp.int32, shape, 1).astype(F32)


def hot(condition):
    return jnp.where(condition, 1.0, 0.0).astype(BF16)


def dot(a, b, contract):
    return lax.dot_general(a, b, (contract, ((), ())), preferred_element_type=F32)


def whole(a, size):
    return jnp.floor((a + 0.5) * (1.0 / size))


def call(kernel, name, out_shape, flops, *args, scalars=None, scratch=(), space=VMEM, limit=LIMIT):
    specs = [space] * len(args)
    if scalars is not None:
        specs = [SMEM] + specs
        args = (scalars,) + args
    return pl.pallas_call(
        kernel,
        in_specs=specs,
        out_shape=out_shape,
        scratch_shapes=scratch,
        compiler_params=pltpu.CompilerParams(vmem_limit_bytes=limit),
        cost_estimate=pl.CostEstimate(flops=flops, bytes_accessed=2**21, transcendentals=0),
        name=name,
    )(*args)


def prepare(members, capacity, *refs):
    sources, (payload, place), scratch = refs[:4], refs[4:6], refs[6:]
    first, second, table, embeddings, sems = scratch
    copies = [
        pltpu.make_async_copy(source, to, sems.at[n])
        for n, (source, to) in enumerate(zip(sources, scratch))
    ]
    for copy in copies:
        copy.start()
    for copy in copies[:3]:
        copy.wait()
    vectors = first.shape[1]
    parts = embeddings.shape[1] // LANES
    slots = table[...]
    local = slots & (LANES - 1)
    owner = (slots // LANES) & (members - 1)
    group = slots // (LANES * members)
    planes = jnp.concatenate([local, owner, group], axis=1).astype(F32).astype(BF16)

    def look_up(ids):
        row = (ids // LANES).astype(F32)
        lane = (ids & (LANES - 1)).astype(F32)
        found = dot(planes, hot(rows_of((table.shape[0], vectors)) == row), ((0,), (0,)))
        mask = rows_of((LANES, vectors)) == lane

        def pick(k):
            return jnp.sum(
                jnp.where(mask, found[k * LANES : (k + 1) * LANES], 0.0), axis=0, keepdims=True
            )

        return pick(0), pick(1), pick(2)

    first_local, first_owner, first_group = look_up(first[...])
    second_local, _, second_group = look_up(second[...])
    is_owner = rows_of((members, vectors)) == first_owner
    before = hot(rows_of((vectors, vectors)) < lanes_of((vectors, vectors)))
    earlier = dot(hot(is_owner), before, ((1,), (0,)))
    rank = jnp.sum(jnp.where(is_owner, earlier, 0.0), axis=0, keepdims=True)
    place[...] = (first_owner * capacity + rank).astype(jnp.int32)
    spot = jnp.where(rank < TILE, first_owner * TILE + rank, rank * members + first_owner)
    order = hot(rows_of((members * capacity, vectors)) == spot)
    copies[3].wait()
    packed = dot(order, embeddings[...], ((1,), (0,)))
    ranked = rows_of((16, vectors)) == rank
    digits = [first_group + 1.0, first_local, second_group + 1.0, second_local]
    spread = [jnp.where(ranked, digit, 0.0) for digit in digits]
    spread.append(jnp.zeros((LANES - 16 * len(digits), vectors), F32))
    labels = dot(hot(is_owner), jnp.concatenate(spread, axis=0).astype(BF16), ((1,), (1,)))
    pieces = [
        packed[: TILE * members, j * LANES : (j + 1) * LANES].reshape(members, TILE, LANES)
        for j in range(parts)
    ]
    rest = [
        packed[p * members : (p + 1) * members, j * LANES : (j + 1) * LANES]
        for p in range(TILE, capacity)
        for j in range(parts)
    ]
    for k in range(0, len(rest), TILE):
        pieces.append(jnp.stack(rest[k : k + TILE], axis=1))
    pieces.append(jnp.broadcast_to(labels[:, None, :], (members, TILE, LANES)))
    payload[...] = jnp.concatenate(pieces, axis=1).astype(BF16)


def spread(capacity, arrived, out):
    members = arrived.shape[0]
    count = members * capacity
    chips, rows, _ = out.shape
    slots = rows - NOTES
    values = arrived[...].astype(F32)
    labels = values[:, capacity * chips].astype(BF16)
    vector = lanes_of((members, slots))
    from_member = jnp.where(
        vector < TILE * members, whole(vector, TILE), vector - members * whole(vector, members)
    )
    found = dot(labels, hot(rows_of((members, slots)) == from_member), ((0,), (0,)))
    vector = lanes_of((16, slots))
    rank = jnp.where(
        vector < TILE * members, vector - TILE * whole(vector, TILE), whole(vector, members)
    )
    ranked = rows_of((16, slots)) == rank
    notes = []
    for k in range(4):
        row = jnp.sum(jnp.where(ranked, found[k * 16 : (k + 1) * 16], 0.0), axis=0, keepdims=True)
        notes += [row[:, q : q + LANES] for q in range(0, slots, LANES)]
    notes.append(jnp.zeros((NOTES - len(notes), LANES), F32))
    notes = jnp.concatenate(notes, axis=0).astype(BF16)
    for j in range(chips):
        out[j, : TILE * members] = (
            values[:, j * TILE : (j + 1) * TILE].reshape(TILE * members, LANES).astype(BF16)
        )
        for p in range(TILE, capacity):
            out[j, p * members : (p + 1) * members] = values[:, p * chips + j].astype(BF16)
        if slots > count:
            out[j, count:slots] = jnp.zeros((slots - count, LANES), BF16)
        out[j, slots:] = notes


def labels_of(slots, notes, k):
    chunks = slots // LANES

    def row(d):
        return jnp.concatenate(
            [notes[d * chunks + q : d * chunks + q + 1] for q in range(chunks)], axis=1
        )

    return row(2 * k) - 1.0, row(2 * k + 1)


def turn(where, old, *outs):
    chips = len(outs)
    for d in range(chips):
        at = lax.rem(where[0] + d, chips)
        outs[d][...] = old[:, pl.ds(pl.multiple_of(at * LANES, LANES), LANES)]


def bare(wide):
    return jnp.concatenate([wide, jnp.ones(wide.shape, BF16)], axis=1)


def pair_of(columns, slots, t):
    both = [columns[2 * t + n, 0:slots] for n in range(2)]
    notes = [columns[2 * t + n, slots:].astype(F32) for n in range(2)]

    def labels(k):
        found = [labels_of(slots, note, k) for note in notes]
        return (
            jnp.concatenate([found[0][0], found[1][0]], axis=1),
            jnp.concatenate([found[0][1], found[1][1]], axis=1),
        )

    return bare(jnp.concatenate(both, axis=0)), labels


def sums(groups, where, columns, *refs):
    olds, (out, total) = refs[:-2], refs[-2:]
    chips, rows, _ = columns.shape
    slots = rows - NOTES
    total[...] = jnp.zeros(total.shape, F32)

    def step(t, _):
        vectors, labels = pair_of(columns, slots, t)
        group, local = labels(0)
        at = hot(rows_of((LANES, 2 * slots)) == local)
        table = jnp.concatenate([at * hot(group == float(g)) for g in range(groups)], axis=0)
        total[...] += dot(table, vectors, ((1,), (0,)))
        return 0

    lax.fori_loop(0, chips // 2, step, 0)
    identity = rows_of((LANES, LANES)) == lanes_of((LANES, LANES))
    counts = []
    for g in range(groups):
        at = slice(g * LANES, (g + 1) * LANES)
        counts.append(
            jnp.sum(jnp.where(identity, total[at, LANES:], 0.0), axis=0, keepdims=True)
        )
    for d, old in enumerate(olds):
        chip = lax.rem(where[0] + chips - d, chips)
        at = pl.ds(pl.multiple_of((2 * chip + where[1]) * LANES, LANES), LANES)
        total[at, :LANES] += old[...].astype(F32)
    out[: groups * LANES] = total[:, :LANES].astype(BF16)
    counts = jnp.concatenate(counts, axis=0)
    high = whole(counts, 256)
    out[groups * LANES : groups * (LANES + 1)] = (counts - 256.0 * high).astype(BF16)
    out[groups * (LANES + 1) :] = high.astype(BF16)


def refit(groups, where, mine, theirs, parts, lists_of):
    lists = groups * LANES

    def counts_of(sums):
        low = sums[lists : lists + groups].astype(F32)
        return low + 256.0 * sums[lists + groups :].astype(F32)

    counts = counts_of(mine) + counts_of(theirs) + 1.0
    identity = rows_of((LANES, LANES)) == lanes_of((LANES, LANES))
    lane = lanes_of((LANES, LANES))
    values = []
    for g in range(groups):
        at = slice(g * LANES, (g + 1) * LANES)
        divisor = jnp.sum(jnp.where(identity, counts[g : g + 1], 0.0), axis=1, keepdims=True)
        total = mine[at].astype(F32) + theirs[at].astype(F32)
        value = (total / divisor).astype(BF16).astype(F32)
        values.append(value)
        size = jnp.sum(value * value, axis=1, keepdims=True)
        one = size.astype(BF16).astype(F32)
        two = (size - one).astype(BF16).astype(F32)
        three = size - one - two
        sizes = jnp.where(lane == 0.0, one, jnp.where(lane == 1.0, two, 0.0))
        sizes = jnp.where(lane == 2.0, three, sizes)
        lists_of[at] = jnp.concatenate([-2.0 * value, sizes], axis=1).astype(BF16)
    for s in range(groups // 2):
        parts[s] = jnp.where(where[1] == 0, values[2 * s], values[2 * s + 1]).astype(BF16)


def score(groups, columns, lists_of, margins):
    chips, rows, _ = columns.shape
    slots = rows - NOTES

    def step(t, _):
        vectors, labels = pair_of(columns, slots, t)
        distance = dot(lists_of[...], vectors, ((1,), (1,)))

        def pick(k):
            group, local = labels(k)
            found = jnp.zeros((LANES, 2 * slots), F32)
            for g in range(groups):
                found = jnp.where(
                    group == float(g), distance[g * LANES : (g + 1) * LANES], found
                )
            return jnp.where(rows_of((LANES, 2 * slots)) == local, found, 0.0)

        margin = jnp.sum(pick(1) - pick(0), axis=0, keepdims=True)
        margins[pl.ds(2 * t, 1), :] = margin[:, :slots]
        margins[pl.ds(2 * t + 1, 1), :] = margin[:, slots:]
        return 0

    lax.fori_loop(0, chips // 2, step, 0)


def on_device(embeddings, assignment, second_choice, list_slot, old_centroids):
    vectors, width = embeddings.shape
    lists = old_centroids.shape[0]
    members = lax.axis_size("mem")
    chips = lax.axis_size("x")
    capacity = vectors // members + 2
    count = members * capacity

    groups = 2 * chips
    slots = count + -count % LANES

    def across(a):
        return lax.ppermute(a, "core", [(0, 1), (1, 0)])

    def shape(*dims, kind=BF16):
        return jax.ShapeDtypeStruct(dims, kind)

    def exchange(axis, a):
        return lax.all_to_all(a, axis, split_axis=0, concat_axis=0, tiled=True)

    where = jnp.stack([lax.axis_index("x"), lax.axis_index("core")]).astype(jnp.int32)
    payload, place = call(
        functools.partial(prepare, members, capacity),
        "prepare",
        (
            shape(members, capacity * width // LANES + TILE, LANES),
            shape(1, vectors, kind=jnp.int32),
        ),
        2**31,
        assignment.reshape(1, vectors),
        second_choice.reshape(1, vectors),
        list_slot.reshape(-1, LANES),
        embeddings,
        scratch=[
            pltpu.VMEM((1, vectors), jnp.int32),
            pltpu.VMEM((1, vectors), jnp.int32),
            pltpu.VMEM((list_slot.shape[0] // LANES, LANES), jnp.int32),
            pltpu.VMEM((vectors, width), BF16),
            pltpu.SemaphoreType.DMA((4,)),
        ],
        space=pl.BlockSpec(memory_space=pl.ANY),
        limit=60 * 2**20,
    )
    arrived = exchange("mem", payload)
    turned = call(turn, "turn", [shape(lists, LANES)] * chips, 2**20, old_centroids, scalars=where)
    olds = [turned[0]]
    for d in range(1, chips):
        olds.append(lax.ppermute(turned[d], "x", [(i, (i + d) % chips) for i in range(chips)]))
    sent = call(
        functools.partial(spread, capacity),
        "spread",
        shape(chips, slots + NOTES, LANES),
        2**24,
        arrived,
    )
    columns = exchange("x", sent)
    mine = call(
        functools.partial(sums, groups),
        "sums",
        shape(groups * (LANES + 2), LANES),
        2**32,
        columns,
        *olds,
        scalars=where,
        scratch=[pltpu.VMEM((groups * LANES, 2 * LANES), F32)],
    )
    parts, lists_of = call(
        functools.partial(refit, groups),
        "refit",
        (shape(chips, lists, LANES), shape(groups * LANES, 2 * LANES)),
        2**24,
        mine,
        across(mine),
        scalars=where,
    )
    returned_parts = exchange("x", parts)
    scores = call(
        functools.partial(score, groups),
        "score",
        shape(chips, slots, kind=F32),
        2**33,
        columns,
        lists_of,
    )
    scores, returned_parts = lax.optimization_barrier((scores, returned_parts))
    fresh = returned_parts.swapaxes(0, 1).reshape(lists, width)
    scores = exchange("x", scores.reshape(chips, 1, slots))
    margin = jnp.sum(scores.reshape(chips, slots), axis=0) * (1.0 / width)
    margin = jnp.concatenate(
        [
            margin[: TILE * members].reshape(members, TILE),
            margin[TILE * members : count].reshape(capacity - TILE, members).T,
        ],
        axis=1,
    )
    returned = exchange("mem", margin.reshape(members, 1, capacity))
    spots = jnp.arange(count, dtype=jnp.int32)
    margins = jnp.sum(
        jnp.where(place.reshape(vectors, 1) == spots[None, :], returned.reshape(1, count), 0.0),
        axis=1,
    )
    return fresh, margins


def solution(mesh):
    groups, members = mesh.devices.shape
    chip_mesh = Mesh(mesh.devices.reshape(groups // 2, 2, members), ("x", "core", "mem"))
    everywhere = ("x", "core", "mem")
    placed = (
        P(everywhere, None),
        P(everywhere),
        P(everywhere),
        P(),
        P(everywhere, None),
    )
    return jax.shard_map(
        on_device,
        mesh=chip_mesh,
        in_specs=placed,
        out_specs=(P(everywhere, None), P(everywhere)),
        check_vma=False,
    )
```

```python
import functools

import jax
import jax.numpy as jnp
from jax import lax
from jax.experimental import pallas as pl
from jax.experimental.pallas import tpu as pltpu
from jax.sharding import Mesh
from jax.sharding import PartitionSpec as P

F32 = jnp.float32
BF16 = jnp.bfloat16
LANES = 128
TILE = 8
NOTES = 32
LIMIT = 40 * 2**20
SMEM = pl.BlockSpec(memory_space=pltpu.SMEM)
VMEM = pl.BlockSpec(memory_space=pltpu.VMEM)


def rows_of(shape):
    return lax.broadcasted_iota(jnp.int32, shape, 0).astype(F32)


def lanes_of(shape):
    return lax.broadcasted_iota(jnp.int32, shape, 1).astype(F32)


def hot(condition):
    return jnp.where(condition, 1.0, 0.0).astype(BF16)


def dot(a, b, contract):
    return lax.dot_general(a, b, (contract, ((), ())), preferred_element_type=F32)


def whole(a, size):
    return jnp.floor((a + 0.5) * (1.0 / size))


def call(kernel, name, out_shape, flops, *args, scalars=None, scratch=(), space=VMEM, limit=LIMIT):
    specs = [space] * len(args)
    if scalars is not None:
        specs = [SMEM] + specs
        args = (scalars,) + args
    return pl.pallas_call(
        kernel,
        in_specs=specs,
        out_shape=out_shape,
        scratch_shapes=scratch,
        compiler_params=pltpu.CompilerParams(vmem_limit_bytes=limit),
        cost_estimate=pl.CostEstimate(flops=flops, bytes_accessed=2**21, transcendentals=0),
        name=name,
    )(*args)


def prepare(members, capacity, *refs):
    sources, (payload, place), scratch = refs[:4], refs[4:6], refs[6:]
    first, second, table, embeddings, sems = scratch
    copies = [
        pltpu.make_async_copy(source, to, sems.at[n])
        for n, (source, to) in enumerate(zip(sources, scratch))
    ]
    for copy in copies:
        copy.start()
    for copy in copies[:3]:
        copy.wait()
    vectors = first.shape[1]
    parts = embeddings.shape[1] // LANES
    slots = table[...]
    local = slots & (LANES - 1)
    owner = (slots // LANES) & (members - 1)
    group = slots // (LANES * members)
    planes = jnp.concatenate([local, owner, group], axis=1).astype(F32).astype(BF16)

    def look_up(ids):
        row = (ids // LANES).astype(F32)
        lane = (ids & (LANES - 1)).astype(F32)
        found = dot(planes, hot(rows_of((table.shape[0], vectors)) == row), ((0,), (0,)))
        mask = rows_of((LANES, vectors)) == lane

        def pick(k):
            return jnp.sum(
                jnp.where(mask, found[k * LANES : (k + 1) * LANES], 0.0), axis=0, keepdims=True
            )

        return pick(0), pick(1), pick(2)

    first_local, first_owner, first_group = look_up(first[...])
    second_local, _, second_group = look_up(second[...])
    is_owner = rows_of((members, vectors)) == first_owner
    before = hot(rows_of((vectors, vectors)) < lanes_of((vectors, vectors)))
    earlier = dot(hot(is_owner), before, ((1,), (0,)))
    rank = jnp.sum(jnp.where(is_owner, earlier, 0.0), axis=0, keepdims=True)
    place[...] = (first_owner * capacity + rank).astype(jnp.int32)
    spot = jnp.where(rank < TILE, first_owner * TILE + rank, rank * members + first_owner)
    order = hot(rows_of((members * capacity, vectors)) == spot)
    copies[3].wait()
    packed = dot(order, embeddings[...], ((1,), (0,)))
    ranked = rows_of((16, vectors)) == rank
    digits = [first_group + 1.0, first_local, second_group + 1.0, second_local]
    spread = [jnp.where(ranked, digit, 0.0) for digit in digits]
    spread.append(jnp.zeros((LANES - 16 * len(digits), vectors), F32))
    labels = dot(hot(is_owner), jnp.concatenate(spread, axis=0).astype(BF16), ((1,), (1,)))
    pieces = [
        packed[: TILE * members, j * LANES : (j + 1) * LANES].reshape(members, TILE, LANES)
        for j in range(parts)
    ]
    rest = [
        packed[p * members : (p + 1) * members, j * LANES : (j + 1) * LANES]
        for p in range(TILE, capacity)
        for j in range(parts)
    ]
    for k in range(0, len(rest), TILE):
        pieces.append(jnp.stack(rest[k : k + TILE], axis=1))
    pieces.append(jnp.broadcast_to(labels[:, None, :], (members, TILE, LANES)))
    payload[...] = jnp.concatenate(pieces, axis=1).astype(BF16)


def spread(capacity, arrived, out):
    members = arrived.shape[0]
    count = members * capacity
    chips, rows, _ = out.shape
    slots = rows - NOTES
    values = arrived[...].astype(F32)
    labels = values[:, capacity * chips].astype(BF16)
    vector = lanes_of((members, slots))
    from_member = jnp.where(
        vector < TILE * members, whole(vector, TILE), vector - members * whole(vector, members)
    )
    found = dot(labels, hot(rows_of((members, slots)) == from_member), ((0,), (0,)))
    vector = lanes_of((16, slots))
    rank = jnp.where(
        vector < TILE * members, vector - TILE * whole(vector, TILE), whole(vector, members)
    )
    ranked = rows_of((16, slots)) == rank
    notes = []
    for k in range(4):
        row = jnp.sum(jnp.where(ranked, found[k * 16 : (k + 1) * 16], 0.0), axis=0, keepdims=True)
        notes += [row[:, q : q + LANES] for q in range(0, slots, LANES)]
    notes.append(jnp.zeros((NOTES - len(notes), LANES), F32))
    notes = jnp.concatenate(notes, axis=0).astype(BF16)
    for j in range(chips):
        out[j, : TILE * members] = (
            values[:, j * TILE : (j + 1) * TILE].reshape(TILE * members, LANES).astype(BF16)
        )
        for p in range(TILE, capacity):
            out[j, p * members : (p + 1) * members] = values[:, p * chips + j].astype(BF16)
        if slots > count:
            out[j, count:slots] = jnp.zeros((slots - count, LANES), BF16)
        out[j, slots:] = notes


def labels_of(slots, notes, k):
    chunks = slots // LANES

    def row(d):
        return jnp.concatenate(
            [notes[d * chunks + q : d * chunks + q + 1] for q in range(chunks)], axis=1
        )

    return row(2 * k) - 1.0, row(2 * k + 1)


def turn(where, old, *outs):
    chips = len(outs)
    for d in range(chips):
        at = lax.rem(where[0] + d, chips)
        outs[d][...] = old[:, pl.ds(pl.multiple_of(at * LANES, LANES), LANES)]


def bare(wide):
    return jnp.concatenate([wide, jnp.ones(wide.shape, BF16)], axis=1)


def pair_of(columns, slots, t):
    both = [columns[2 * t + n, 0:slots] for n in range(2)]
    notes = [columns[2 * t + n, slots:].astype(F32) for n in range(2)]

    def labels(k):
        found = [labels_of(slots, note, k) for note in notes]
        return (
            jnp.concatenate([found[0][0], found[1][0]], axis=1),
            jnp.concatenate([found[0][1], found[1][1]], axis=1),
        )

    return bare(jnp.concatenate(both, axis=0)), labels


def sums(groups, where, columns, *refs):
    olds, (out, total) = refs[:-2], refs[-2:]
    chips, rows, _ = columns.shape
    slots = rows - NOTES
    total[...] = jnp.zeros(total.shape, F32)

    def step(t, _):
        vectors, labels = pair_of(columns, slots, t)
        group, local = labels(0)
        at = hot(rows_of((LANES, 2 * slots)) == local)
        table = jnp.concatenate([at * hot(group == float(g)) for g in range(groups)], axis=0)
        total[...] += dot(table, vectors, ((1,), (0,)))
        return 0

    lax.fori_loop(0, chips // 2, step, 0)
    identity = rows_of((LANES, LANES)) == lanes_of((LANES, LANES))
    counts = []
    for g in range(groups):
        at = slice(g * LANES, (g + 1) * LANES)
        counts.append(
            jnp.sum(jnp.where(identity, total[at, LANES:], 0.0), axis=0, keepdims=True)
        )
    for d, old in enumerate(olds):
        chip = lax.rem(where[0] + chips - d, chips)
        at = pl.ds(pl.multiple_of((2 * chip + where[1]) * LANES, LANES), LANES)
        total[at, :LANES] += old[...].astype(F32)
    out[: groups * LANES] = total[:, :LANES].astype(BF16)
    counts = jnp.concatenate(counts, axis=0)
    high = whole(counts, 256)
    out[groups * LANES : groups * (LANES + 1)] = (counts - 256.0 * high).astype(BF16)
    out[groups * (LANES + 1) :] = high.astype(BF16)


def refit(groups, where, mine, theirs, parts, lists_of):
    lists = groups * LANES

    def counts_of(sums):
        low = sums[lists : lists + groups].astype(F32)
        return low + 256.0 * sums[lists + groups :].astype(F32)

    counts = counts_of(mine) + counts_of(theirs) + 1.0
    identity = rows_of((LANES, LANES)) == lanes_of((LANES, LANES))
    lane = lanes_of((LANES, LANES))
    values = []
    for g in range(groups):
        at = slice(g * LANES, (g + 1) * LANES)
        divisor = jnp.sum(jnp.where(identity, counts[g : g + 1], 0.0), axis=1, keepdims=True)
        total = mine[at].astype(F32) + theirs[at].astype(F32)
        value = (total / divisor).astype(BF16).astype(F32)
        values.append(value)
        size = jnp.sum(value * value, axis=1, keepdims=True)
        one = size.astype(BF16).astype(F32)
        two = (size - one).astype(BF16).astype(F32)
        three = size - one - two
        sizes = jnp.where(lane == 0.0, one, jnp.where(lane == 1.0, two, 0.0))
        sizes = jnp.where(lane == 2.0, three, sizes)
        lists_of[at] = jnp.concatenate([-2.0 * value, sizes], axis=1).astype(BF16)
    for s in range(groups // 2):
        parts[s] = jnp.where(where[1] == 0, values[2 * s], values[2 * s + 1]).astype(BF16)


def score(groups, columns, lists_of, margins):
    chips, rows, _ = columns.shape
    slots = rows - NOTES

    def step(t, _):
        vectors, labels = pair_of(columns, slots, t)
        distance = dot(lists_of[...], vectors, ((1,), (1,)))

        def pick(k):
            group, local = labels(k)
            found = jnp.zeros((LANES, 2 * slots), F32)
            for g in range(groups):
                found = jnp.where(
                    group == float(g), distance[g * LANES : (g + 1) * LANES], found
                )
            return jnp.where(rows_of((LANES, 2 * slots)) == local, found, 0.0)

        margin = jnp.sum(pick(1) - pick(0), axis=0, keepdims=True)
        margins[pl.ds(2 * t, 1), :] = margin[:, :slots]
        margins[pl.ds(2 * t + 1, 1), :] = margin[:, slots:]
        return 0

    lax.fori_loop(0, chips // 2, step, 0)


def on_device(embeddings, assignment, second_choice, list_slot, old_centroids):
    vectors, width = embeddings.shape
    lists = old_centroids.shape[0]
    members = lax.axis_size("mem")
    chips = lax.axis_size("x")
    capacity = vectors // members + 2
    count = members * capacity

    groups = 2 * chips
    slots = count + -count % LANES

    def across(a):
        return lax.ppermute(a, "core", [(0, 1), (1, 0)])

    def shape(*dims, kind=BF16):
        return jax.ShapeDtypeStruct(dims, kind)

    def exchange(axis, a):
        return lax.all_to_all(a, axis, split_axis=0, concat_axis=0, tiled=True)

    where = jnp.stack([lax.axis_index("x"), lax.axis_index("core")]).astype(jnp.int32)
    payload, place = call(
        functools.partial(prepare, members, capacity),
        "prepare",
        (
            shape(members, capacity * width // LANES + TILE, LANES),
            shape(1, vectors, kind=jnp.int32),
        ),
        2**31,
        assignment.reshape(1, vectors),
        second_choice.reshape(1, vectors),
        list_slot.reshape(-1, LANES),
        embeddings,
        scratch=[
            pltpu.VMEM((1, vectors), jnp.int32),
            pltpu.VMEM((1, vectors), jnp.int32),
            pltpu.VMEM((list_slot.shape[0] // LANES, LANES), jnp.int32),
            pltpu.VMEM((vectors, width), BF16),
            pltpu.SemaphoreType.DMA((4,)),
        ],
        space=pl.BlockSpec(memory_space=pl.ANY),
        limit=60 * 2**20,
    )
    arrived = exchange("mem", payload)
    turned = call(turn, "turn", [shape(lists, LANES)] * chips, 2**20, old_centroids, scalars=where)
    olds = [turned[0]]
    for d in range(1, chips):
        olds.append(lax.ppermute(turned[d], "x", [(i, (i + d) % chips) for i in range(chips)]))
    arrived, *olds = lax.optimization_barrier((arrived, *olds))
    sent = call(
        functools.partial(spread, capacity),
        "spread",
        shape(chips, slots + NOTES, LANES),
        2**24,
        arrived,
    )
    columns = exchange("x", sent)
    mine = call(
        functools.partial(sums, groups),
        "sums",
        shape(groups * (LANES + 2), LANES),
        2**32,
        columns,
        *olds,
        scalars=where,
        scratch=[pltpu.VMEM((groups * LANES, 2 * LANES), F32)],
    )
    parts, lists_of = call(
        functools.partial(refit, groups),
        "refit",
        (shape(chips, lists, LANES), shape(groups * LANES, 2 * LANES)),
        2**24,
        mine,
        across(mine),
        scalars=where,
    )
    returned_parts = exchange("x", parts)
    scores = call(
        functools.partial(score, groups),
        "score",
        shape(chips, slots, kind=F32),
        2**33,
        columns,
        lists_of,
    )
    scores, returned_parts = lax.optimization_barrier((scores, returned_parts))
    fresh = returned_parts.swapaxes(0, 1).reshape(lists, width)
    scores = exchange("x", scores.reshape(chips, 1, slots))
    margin = jnp.sum(scores.reshape(chips, slots), axis=0) * (1.0 / width)
    margin = jnp.concatenate(
        [
            margin[: TILE * members].reshape(members, TILE),
            margin[TILE * members : count].reshape(capacity - TILE, members).T,
        ],
        axis=1,
    )
    returned = exchange("mem", margin.reshape(members, 1, capacity))
    spots = jnp.arange(count, dtype=jnp.int32)
    margins = jnp.sum(
        jnp.where(place.reshape(vectors, 1) == spots[None, :], returned.reshape(1, count), 0.0),
        axis=1,
    )
    return fresh, margins


def solution(mesh):
    groups, members = mesh.devices.shape
    chip_mesh = Mesh(mesh.devices.reshape(groups // 2, 2, members), ("x", "core", "mem"))
    everywhere = ("x", "core", "mem")
    placed = (
        P(everywhere, None),
        P(everywhere),
        P(everywhere),
        P(),
        P(everywhere, None),
    )
    return jax.shard_map(
        on_device,
        mesh=chip_mesh,
        in_specs=placed,
        out_specs=(P(everywhere, None), P(everywhere)),
        check_vma=False,
    )
```

```python
import functools

import jax
import jax.numpy as jnp
from jax import lax
from jax.experimental import pallas as pl
from jax.experimental.pallas import tpu as pltpu
from jax.sharding import Mesh
from jax.sharding import PartitionSpec as P

F32 = jnp.float32
BF16 = jnp.bfloat16
LANES = 128
TILE = 8
BLOCK = 16
NOTES = 32
LIMIT = 40 * 2**20
SMEM = pl.BlockSpec(memory_space=pltpu.SMEM)
VMEM = pl.BlockSpec(memory_space=pltpu.VMEM)


def rows_of(shape):
    return lax.broadcasted_iota(jnp.int32, shape, 0).astype(F32)


def lanes_of(shape):
    return lax.broadcasted_iota(jnp.int32, shape, 1).astype(F32)


def hot(condition):
    return jnp.where(condition, 1.0, 0.0).astype(BF16)


def dot(a, b, contract):
    return lax.dot_general(a, b, (contract, ((), ())), preferred_element_type=F32)


def whole(a, size):
    return jnp.floor((a + 0.5) * (1.0 / size))


def call(kernel, name, out_shape, flops, *args, scalars=None, scratch=(), space=VMEM, limit=LIMIT):
    specs = [space] * len(args)
    if scalars is not None:
        specs = [SMEM] + specs
        args = (scalars,) + args
    return pl.pallas_call(
        kernel,
        in_specs=specs,
        out_shape=out_shape,
        scratch_shapes=scratch,
        compiler_params=pltpu.CompilerParams(vmem_limit_bytes=limit),
        cost_estimate=pl.CostEstimate(flops=flops, bytes_accessed=2**21, transcendentals=0),
        name=name,
    )(*args)


def prepare(members, capacity, *refs):
    sources, (payload, place), scratch = refs[:4], refs[4:6], refs[6:]
    first, second, table, embeddings, sems = scratch
    copies = [
        pltpu.make_async_copy(source, to, sems.at[n])
        for n, (source, to) in enumerate(zip(sources, scratch))
    ]
    for copy in copies:
        copy.start()
    for copy in copies[:3]:
        copy.wait()
    vectors = first.shape[1]
    slots = table[...]
    local = slots & (LANES - 1)
    owner = (slots // LANES) & (members - 1)
    group = slots // (LANES * members)
    planes = jnp.concatenate([local, owner, group], axis=1).astype(F32).astype(BF16)

    def look_up(ids):
        row = (ids // LANES).astype(F32)
        lane = (ids & (LANES - 1)).astype(F32)
        found = dot(planes, hot(rows_of((table.shape[0], vectors)) == row), ((0,), (0,)))
        mask = rows_of((LANES, vectors)) == lane

        def pick(k):
            return jnp.sum(
                jnp.where(mask, found[k * LANES : (k + 1) * LANES], 0.0), axis=0, keepdims=True
            )

        return pick(0), pick(1), pick(2)

    first_local, first_owner, first_group = look_up(first[...])
    second_local, _, second_group = look_up(second[...])
    is_owner = rows_of((members, vectors)) == first_owner
    before = hot(rows_of((vectors, vectors)) < lanes_of((vectors, vectors)))
    earlier = dot(hot(is_owner), before, ((1,), (0,)))
    rank = jnp.sum(jnp.where(is_owner, earlier, 0.0), axis=0, keepdims=True)
    place[...] = (first_owner * capacity + rank).astype(jnp.int32)
    spot = jnp.where(rank < TILE, first_owner * TILE + rank, rank * members + first_owner)
    order = hot(rows_of((members * capacity, vectors)) == spot)
    copies[3].wait()
    packed = dot(order, embeddings[...], ((1,), (0,)))
    ranked = rows_of((16, vectors)) == rank
    digits = [first_group + 1.0, first_local, second_group + 1.0, second_local]
    spread = [jnp.where(ranked, digit, 0.0) for digit in digits]
    spread.append(jnp.zeros((LANES - 16 * len(digits), vectors), F32))
    labels = dot(hot(is_owner), jnp.concatenate(spread, axis=0).astype(BF16), ((1,), (1,)))
    empty = [jnp.zeros((members, LANES), F32)] * (BLOCK - capacity - 1)
    for j in range(embeddings.shape[1] // LANES):
        at = slice(j * LANES, (j + 1) * LANES)
        rest = [packed[p * members : (p + 1) * members, at] for p in range(TILE, capacity)]
        block = [
            packed[: TILE * members, at].reshape(members, TILE, LANES),
            jnp.stack(rest + [labels] + empty, axis=1),
        ]
        payload[j * members : (j + 1) * members] = jnp.concatenate(block, axis=1).astype(BF16)


def gather(capacity, arrived, out):
    chips, rows, _ = out.shape
    members = arrived.shape[0] // chips
    count = members * capacity
    slots = rows - NOTES
    vector = lanes_of((members, slots))
    from_member = jnp.where(
        vector < TILE * members, whole(vector, TILE), vector - members * whole(vector, members)
    )
    from_member = hot(rows_of((members, slots)) == from_member)
    vector = lanes_of((16, slots))
    rank = jnp.where(
        vector < TILE * members, vector - TILE * whole(vector, TILE), whole(vector, members)
    )
    ranked = rows_of((16, slots)) == rank
    for s in range(chips):
        values = arrived[s * members : (s + 1) * members].astype(F32)
        out[s, : TILE * members] = (
            values[:, :TILE].reshape(TILE * members, LANES).astype(BF16)
        )
        for p in range(TILE, capacity):
            out[s, p * members : (p + 1) * members] = values[:, p].astype(BF16)
        if slots > count:
            out[s, count:slots] = jnp.zeros((slots - count, LANES), BF16)
        found = dot(values[:, capacity].astype(BF16), from_member, ((0,), (0,)))
        notes = []
        for k in range(4):
            row = jnp.where(ranked, found[k * 16 : (k + 1) * 16], 0.0)
            row = jnp.sum(row, axis=0, keepdims=True)
            notes += [row[:, q : q + LANES] for q in range(0, slots, LANES)]
        notes.append(jnp.zeros((NOTES - len(notes), LANES), F32))
        out[s, slots:] = jnp.concatenate(notes, axis=0).astype(BF16)


def labels_of(slots, notes, k):
    chunks = slots // LANES

    def row(d):
        return jnp.concatenate(
            [notes[d * chunks + q : d * chunks + q + 1] for q in range(chunks)], axis=1
        )

    return row(2 * k) - 1.0, row(2 * k + 1)


def turn(where, old, *outs):
    chips = len(outs)
    for d in range(chips):
        at = lax.rem(where[0] + d, chips)
        outs[d][...] = old[:, pl.ds(pl.multiple_of(at * LANES, LANES), LANES)]


def bare(wide):
    return jnp.concatenate([wide, jnp.ones(wide.shape, BF16)], axis=1)


def pair_of(columns, slots, t):
    both = [columns[2 * t + n, 0:slots] for n in range(2)]
    notes = [columns[2 * t + n, slots:].astype(F32) for n in range(2)]

    def labels(k):
        found = [labels_of(slots, note, k) for note in notes]
        return (
            jnp.concatenate([found[0][0], found[1][0]], axis=1),
            jnp.concatenate([found[0][1], found[1][1]], axis=1),
        )

    return bare(jnp.concatenate(both, axis=0)), labels


def sums(groups, where, columns, *refs):
    olds, (out, total) = refs[:-2], refs[-2:]
    chips, rows, _ = columns.shape
    slots = rows - NOTES
    total[...] = jnp.zeros(total.shape, F32)

    def step(t, _):
        vectors, labels = pair_of(columns, slots, t)
        group, local = labels(0)
        at = hot(rows_of((LANES, 2 * slots)) == local)
        table = jnp.concatenate([at * hot(group == float(g)) for g in range(groups)], axis=0)
        total[...] += dot(table, vectors, ((1,), (0,)))
        return 0

    lax.fori_loop(0, chips // 2, step, 0)
    identity = rows_of((LANES, LANES)) == lanes_of((LANES, LANES))
    counts = []
    for g in range(groups):
        at = slice(g * LANES, (g + 1) * LANES)
        counts.append(
            jnp.sum(jnp.where(identity, total[at, LANES:], 0.0), axis=0, keepdims=True)
        )
    for d, old in enumerate(olds):
        chip = lax.rem(where[0] + chips - d, chips)
        at = pl.ds(pl.multiple_of((2 * chip + where[1]) * LANES, LANES), LANES)
        total[at, :LANES] += old[...].astype(F32)
    out[: groups * LANES] = total[:, :LANES].astype(BF16)
    counts = jnp.concatenate(counts, axis=0)
    high = whole(counts, 256)
    out[groups * LANES : groups * (LANES + 1)] = (counts - 256.0 * high).astype(BF16)
    out[groups * (LANES + 1) :] = high.astype(BF16)


def refit(groups, where, mine, theirs, parts, lists_of):
    lists = groups * LANES

    def counts_of(sums):
        low = sums[lists : lists + groups].astype(F32)
        return low + 256.0 * sums[lists + groups :].astype(F32)

    counts = counts_of(mine) + counts_of(theirs) + 1.0
    identity = rows_of((LANES, LANES)) == lanes_of((LANES, LANES))
    lane = lanes_of((LANES, LANES))
    values = []
    for g in range(groups):
        at = slice(g * LANES, (g + 1) * LANES)
        divisor = jnp.sum(jnp.where(identity, counts[g : g + 1], 0.0), axis=1, keepdims=True)
        total = mine[at].astype(F32) + theirs[at].astype(F32)
        value = (total / divisor).astype(BF16).astype(F32)
        values.append(value)
        size = jnp.sum(value * value, axis=1, keepdims=True)
        one = size.astype(BF16).astype(F32)
        two = (size - one).astype(BF16).astype(F32)
        three = size - one - two
        sizes = jnp.where(lane == 0.0, one, jnp.where(lane == 1.0, two, 0.0))
        sizes = jnp.where(lane == 2.0, three, sizes)
        lists_of[at] = jnp.concatenate([-2.0 * value, sizes], axis=1).astype(BF16)
    for s in range(groups // 2):
        parts[s] = jnp.where(where[1] == 0, values[2 * s], values[2 * s + 1]).astype(BF16)


def score(groups, columns, lists_of, margins):
    chips, rows, _ = columns.shape
    slots = rows - NOTES

    def step(t, _):
        vectors, labels = pair_of(columns, slots, t)
        distance = dot(lists_of[...], vectors, ((1,), (1,)))

        def pick(k):
            group, local = labels(k)
            found = jnp.zeros((LANES, 2 * slots), F32)
            for g in range(groups):
                found = jnp.where(
                    group == float(g), distance[g * LANES : (g + 1) * LANES], found
                )
            return jnp.where(rows_of((LANES, 2 * slots)) == local, found, 0.0)

        margin = jnp.sum(pick(1) - pick(0), axis=0, keepdims=True)
        margins[pl.ds(2 * t, 1), :] = margin[:, :slots]
        margins[pl.ds(2 * t + 1, 1), :] = margin[:, slots:]
        return 0

    lax.fori_loop(0, chips // 2, step, 0)


def on_device(embeddings, assignment, second_choice, list_slot, old_centroids):
    vectors, width = embeddings.shape
    lists = old_centroids.shape[0]
    members = lax.axis_size("mem")
    chips = lax.axis_size("x")
    capacity = vectors // members + 2
    count = members * capacity

    groups = 2 * chips
    slots = count + -count % LANES

    def across(a):
        return lax.ppermute(a, "core", [(0, 1), (1, 0)])

    def shape(*dims, kind=BF16):
        return jax.ShapeDtypeStruct(dims, kind)

    def exchange(axis, a):
        return lax.all_to_all(a, axis, split_axis=0, concat_axis=0, tiled=True)

    where = jnp.stack([lax.axis_index("x"), lax.axis_index("core")]).astype(jnp.int32)
    payload, place = call(
        functools.partial(prepare, members, capacity),
        "prepare",
        (
            shape(chips * members, BLOCK, LANES),
            shape(1, vectors, kind=jnp.int32),
        ),
        2**31,
        assignment.reshape(1, vectors),
        second_choice.reshape(1, vectors),
        list_slot.reshape(-1, LANES),
        embeddings,
        scratch=[
            pltpu.VMEM((1, vectors), jnp.int32),
            pltpu.VMEM((1, vectors), jnp.int32),
            pltpu.VMEM((list_slot.shape[0] // LANES, LANES), jnp.int32),
            pltpu.VMEM((vectors, width), BF16),
            pltpu.SemaphoreType.DMA((4,)),
        ],
        space=pl.BlockSpec(memory_space=pl.ANY),
        limit=60 * 2**20,
    )
    arrived = exchange(("x", "mem"), payload)
    turned = call(turn, "turn", [shape(lists, LANES)] * chips, 2**20, old_centroids, scalars=where)
    olds = [turned[0]]
    for d in range(1, chips):
        olds.append(lax.ppermute(turned[d], "x", [(i, (i + d) % chips) for i in range(chips)]))
    arrived, *olds = lax.optimization_barrier((arrived, *olds))
    columns = call(
        functools.partial(gather, capacity),
        "gather",
        shape(chips, slots + NOTES, LANES),
        2**24,
        arrived,
    )
    mine = call(
        functools.partial(sums, groups),
        "sums",
        shape(groups * (LANES + 2), LANES),
        2**32,
        columns,
        *olds,
        scalars=where,
        scratch=[pltpu.VMEM((groups * LANES, 2 * LANES), F32)],
    )
    parts, lists_of = call(
        functools.partial(refit, groups),
        "refit",
        (shape(chips, lists, LANES), shape(groups * LANES, 2 * LANES)),
        2**24,
        mine,
        across(mine),
        scalars=where,
    )
    returned_parts = exchange("x", parts)
    scores = call(
        functools.partial(score, groups),
        "score",
        shape(chips, slots, kind=F32),
        2**33,
        columns,
        lists_of,
    )
    scores, returned_parts = lax.optimization_barrier((scores, returned_parts))
    fresh = returned_parts.swapaxes(0, 1).reshape(lists, width)
    scores = exchange("x", scores.reshape(chips, 1, slots))
    margin = jnp.sum(scores.reshape(chips, slots), axis=0) * (1.0 / width)
    margin = jnp.concatenate(
        [
            margin[: TILE * members].reshape(members, TILE),
            margin[TILE * members : count].reshape(capacity - TILE, members).T,
        ],
        axis=1,
    )
    returned = exchange("mem", margin.reshape(members, 1, capacity))
    spots = jnp.arange(count, dtype=jnp.int32)
    margins = jnp.sum(
        jnp.where(place.reshape(vectors, 1) == spots[None, :], returned.reshape(1, count), 0.0),
        axis=1,
    )
    return fresh, margins


def solution(mesh):
    groups, members = mesh.devices.shape
    chip_mesh = Mesh(mesh.devices.reshape(groups // 2, 2, members), ("x", "core", "mem"))
    everywhere = ("x", "core", "mem")
    placed = (
        P(everywhere, None),
        P(everywhere),
        P(everywhere),
        P(),
        P(everywhere, None),
    )
    return jax.shard_map(
        on_device,
        mesh=chip_mesh,
        in_specs=placed,
        out_specs=(P(everywhere, None), P(everywhere)),
        check_vma=False,
    )
```

```python
import functools

import jax
import jax.numpy as jnp
from jax import lax
from jax.experimental import pallas as pl
from jax.experimental.pallas import tpu as pltpu
from jax.sharding import Mesh
from jax.sharding import PartitionSpec as P

F32 = jnp.float32
BF16 = jnp.bfloat16
LANES = 128
TILE = 8
BLOCK = 16
NOTES = 32
LIMIT = 28 * 2**20
SMEM = pl.BlockSpec(memory_space=pltpu.SMEM)
VMEM = pl.BlockSpec(memory_space=pltpu.VMEM)


def rows_of(shape):
    return lax.broadcasted_iota(jnp.int32, shape, 0).astype(F32)


def lanes_of(shape):
    return lax.broadcasted_iota(jnp.int32, shape, 1).astype(F32)


def hot(condition):
    return jnp.where(condition, 1.0, 0.0).astype(BF16)


def dot(a, b, contract):
    return lax.dot_general(a, b, (contract, ((), ())), preferred_element_type=F32)


def whole(a, size):
    return jnp.floor((a + 0.5) * (1.0 / size))


def call(kernel, name, out_shape, flops, *args, scalars=None, scratch=(), space=VMEM, limit=LIMIT):
    specs = [space] * len(args)
    if scalars is not None:
        specs = [SMEM] + specs
        args = (scalars,) + args
    return pl.pallas_call(
        kernel,
        in_specs=specs,
        out_shape=out_shape,
        scratch_shapes=scratch,
        compiler_params=pltpu.CompilerParams(vmem_limit_bytes=limit),
        cost_estimate=pl.CostEstimate(flops=flops, bytes_accessed=2**21, transcendentals=0),
        name=name,
    )(*args)


def prepare(members, capacity, *refs):
    sources, (payload, place), scratch = refs[:4], refs[4:6], refs[6:]
    first, second, table, embeddings, sems = scratch
    copies = [
        pltpu.make_async_copy(source, to, sems.at[n])
        for n, (source, to) in enumerate(zip(sources, scratch))
    ]
    for copy in copies:
        copy.start()
    for copy in copies[:3]:
        copy.wait()
    vectors = first.shape[1]
    slots = table[...]
    local = slots & (LANES - 1)
    owner = (slots // LANES) & (members - 1)
    group = slots // (LANES * members)
    planes = jnp.concatenate([local, owner, group], axis=1).astype(F32).astype(BF16)

    def look_up(ids):
        row = (ids // LANES).astype(F32)
        lane = (ids & (LANES - 1)).astype(F32)
        found = dot(planes, hot(rows_of((table.shape[0], vectors)) == row), ((0,), (0,)))
        mask = rows_of((LANES, vectors)) == lane

        def pick(k):
            return jnp.sum(
                jnp.where(mask, found[k * LANES : (k + 1) * LANES], 0.0), axis=0, keepdims=True
            )

        return pick(0), pick(1), pick(2)

    first_local, first_owner, first_group = look_up(first[...])
    second_local, _, second_group = look_up(second[...])
    is_owner = rows_of((members, vectors)) == first_owner
    before = hot(rows_of((vectors, vectors)) < lanes_of((vectors, vectors)))
    earlier = dot(hot(is_owner), before, ((1,), (0,)))
    rank = jnp.sum(jnp.where(is_owner, earlier, 0.0), axis=0, keepdims=True)
    place[...] = (first_owner * capacity + rank).astype(jnp.int32)
    spot = jnp.where(rank < TILE, first_owner * TILE + rank, rank * members + first_owner)
    order = hot(rows_of((members * capacity, vectors)) == spot)
    copies[3].wait()
    packed = dot(order, embeddings[...], ((1,), (0,)))
    ranked = rows_of((16, vectors)) == rank
    digits = [first_group + 1.0, first_local, second_group + 1.0, second_local]
    spread = [jnp.where(ranked, digit, 0.0) for digit in digits]
    spread.append(jnp.zeros((LANES - 16 * len(digits), vectors), F32))
    labels = dot(hot(is_owner), jnp.concatenate(spread, axis=0).astype(BF16), ((1,), (1,)))
    empty = [jnp.zeros((members, LANES), F32)] * (BLOCK - capacity - 1)
    for j in range(embeddings.shape[1] // LANES):
        at = slice(j * LANES, (j + 1) * LANES)
        rest = [packed[p * members : (p + 1) * members, at] for p in range(TILE, capacity)]
        block = [
            packed[: TILE * members, at].reshape(members, TILE, LANES),
            jnp.stack(rest + [labels] + empty, axis=1),
        ]
        payload[j * members : (j + 1) * members] = jnp.concatenate(block, axis=1).astype(BF16)


def gather(capacity, arrived, out):
    chips, rows, _ = out.shape
    members = arrived.shape[0] // chips
    count = members * capacity
    slots = rows - NOTES
    vector = lanes_of((members, slots))
    from_member = jnp.where(
        vector < TILE * members, whole(vector, TILE), vector - members * whole(vector, members)
    )
    from_member = hot(rows_of((members, slots)) == from_member)
    vector = lanes_of((16, slots))
    rank = jnp.where(
        vector < TILE * members, vector - TILE * whole(vector, TILE), whole(vector, members)
    )
    ranked = rows_of((16, slots)) == rank
    for s in range(chips):
        values = arrived[s * members : (s + 1) * members].astype(F32)
        out[s, : TILE * members] = (
            values[:, :TILE].reshape(TILE * members, LANES).astype(BF16)
        )
        for p in range(TILE, capacity):
            out[s, p * members : (p + 1) * members] = values[:, p].astype(BF16)
        if slots > count:
            out[s, count:slots] = jnp.zeros((slots - count, LANES), BF16)
        found = dot(values[:, capacity].astype(BF16), from_member, ((0,), (0,)))
        notes = []
        for k in range(4):
            row = jnp.where(ranked, found[k * 16 : (k + 1) * 16], 0.0)
            row = jnp.sum(row, axis=0, keepdims=True)
            notes += [row[:, q : q + LANES] for q in range(0, slots, LANES)]
        notes.append(jnp.zeros((NOTES - len(notes), LANES), F32))
        out[s, slots:] = jnp.concatenate(notes, axis=0).astype(BF16)


def labels_of(slots, notes, k):
    chunks = slots // LANES

    def row(d):
        return jnp.concatenate(
            [notes[d * chunks + q : d * chunks + q + 1] for q in range(chunks)], axis=1
        )

    return row(2 * k) - 1.0, row(2 * k + 1)


def turn(chips, where, old, other, near, far, *along):
    def share(a, chip):
        return a[:, pl.ds(pl.multiple_of(chip * LANES, LANES), LANES)]

    near[...] = share(old, where[0])
    far[...] = share(old, lax.rem(where[0] + chips // 2, chips))
    for k, out in enumerate(along, 1):
        chip = lax.rem(where[0] + chips + (1 - 2 * where[1]) * k, chips)
        one, two = share(old, chip).astype(F32), share(other, chip).astype(F32)
        out[:LANES] = jnp.where(where[1] == 0, one, two).astype(BF16)
        out[LANES:] = jnp.where(where[1] == 0, two, one).astype(BF16)


def bare(wide):
    return jnp.concatenate([wide, jnp.ones(wide.shape, BF16)], axis=1)


def pair_of(columns, slots, t):
    both = [columns[2 * t + n, 0:slots] for n in range(2)]
    notes = [columns[2 * t + n, slots:].astype(F32) for n in range(2)]

    def labels(k):
        found = [labels_of(slots, note, k) for note in notes]
        return (
            jnp.concatenate([found[0][0], found[1][0]], axis=1),
            jnp.concatenate([found[0][1], found[1][1]], axis=1),
        )

    return bare(jnp.concatenate(both, axis=0)), labels


def sums(groups, where, columns, *refs):
    olds, (out, total) = refs[:-2], refs[-2:]
    chips, rows, _ = columns.shape
    slots = rows - NOTES
    total[...] = jnp.zeros(total.shape, F32)

    def step(t, _):
        vectors, labels = pair_of(columns, slots, t)
        group, local = labels(0)
        at = hot(rows_of((LANES, 2 * slots)) == local)
        table = jnp.concatenate([at * hot(group == float(g)) for g in range(groups)], axis=0)
        total[...] += dot(table, vectors, ((1,), (0,)))
        return 0

    lax.fori_loop(0, chips // 2, step, 0)
    identity = rows_of((LANES, LANES)) == lanes_of((LANES, LANES))
    counts = []
    for g in range(groups):
        at = slice(g * LANES, (g + 1) * LANES)
        counts.append(
            jnp.sum(jnp.where(identity, total[at, LANES:], 0.0), axis=0, keepdims=True)
        )
    near, far, *along = olds
    for old, chip in ((near, where[0]), (far, lax.rem(where[0] + chips // 2, chips))):
        at = pl.ds(pl.multiple_of((2 * chip + where[1]) * LANES, LANES), LANES)
        total[at, :LANES] += old[...].astype(F32)
    for k, old in enumerate(along, 1):
        chip = lax.rem(where[0] + chips - (1 - 2 * where[1]) * k, chips)
        at = pl.ds(pl.multiple_of(2 * chip * LANES, 2 * LANES), 2 * LANES)
        total[at, :LANES] += old[...].astype(F32)
    out[: groups * LANES] = total[:, :LANES].astype(BF16)
    counts = jnp.concatenate(counts, axis=0)
    high = whole(counts, 256)
    out[groups * LANES : groups * (LANES + 1)] = (counts - 256.0 * high).astype(BF16)
    out[groups * (LANES + 1) :] = high.astype(BF16)


def refit(groups, where, mine, theirs, parts, lists_of):
    lists = groups * LANES

    def counts_of(sums):
        low = sums[lists : lists + groups].astype(F32)
        return low + 256.0 * sums[lists + groups :].astype(F32)

    counts = counts_of(mine) + counts_of(theirs) + 1.0
    identity = rows_of((LANES, LANES)) == lanes_of((LANES, LANES))
    lane = lanes_of((LANES, LANES))
    values = []
    for g in range(groups):
        at = slice(g * LANES, (g + 1) * LANES)
        divisor = jnp.sum(jnp.where(identity, counts[g : g + 1], 0.0), axis=1, keepdims=True)
        total = mine[at].astype(F32) + theirs[at].astype(F32)
        value = (total / divisor).astype(BF16).astype(F32)
        values.append(value)
        size = jnp.sum(value * value, axis=1, keepdims=True)
        one = size.astype(BF16).astype(F32)
        two = (size - one).astype(BF16).astype(F32)
        three = size - one - two
        sizes = jnp.where(lane == 0.0, one, jnp.where(lane == 1.0, two, 0.0))
        sizes = jnp.where(lane == 2.0, three, sizes)
        lists_of[at] = jnp.concatenate([-2.0 * value, sizes], axis=1).astype(BF16)
    for s in range(groups // 2):
        parts[s] = jnp.where(where[1] == 0, values[2 * s], values[2 * s + 1]).astype(BF16)


def score(groups, columns, lists_of, margins):
    chips, rows, _ = columns.shape
    slots = rows - NOTES

    def step(t, _):
        vectors, labels = pair_of(columns, slots, t)
        distance = dot(lists_of[...], vectors, ((1,), (1,)))

        def pick(k):
            group, local = labels(k)
            found = jnp.zeros((LANES, 2 * slots), F32)
            for g in range(groups):
                found = jnp.where(
                    group == float(g), distance[g * LANES : (g + 1) * LANES], found
                )
            return jnp.where(rows_of((LANES, 2 * slots)) == local, found, 0.0)

        margin = jnp.sum(pick(1) - pick(0), axis=0, keepdims=True)
        margins[pl.ds(2 * t, 1), :] = margin[:, :slots]
        margins[pl.ds(2 * t + 1, 1), :] = margin[:, slots:]
        return 0

    lax.fori_loop(0, chips // 2, step, 0)


def on_device(embeddings, assignment, second_choice, list_slot, old_centroids):
    vectors, width = embeddings.shape
    lists = old_centroids.shape[0]
    members = lax.axis_size("mem")
    chips = lax.axis_size("x")
    capacity = vectors // members + 2
    count = members * capacity

    groups = 2 * chips
    slots = count + -count % LANES

    def across(a):
        return lax.ppermute(a, "core", [(0, 1), (1, 0)])

    def shape(*dims, kind=BF16):
        return jax.ShapeDtypeStruct(dims, kind)

    def exchange(axis, a):
        return lax.all_to_all(a, axis, split_axis=0, concat_axis=0, tiled=True)

    where = jnp.stack([lax.axis_index("x"), lax.axis_index("core")]).astype(jnp.int32)
    payload, place = call(
        functools.partial(prepare, members, capacity),
        "prepare",
        (
            shape(chips * members, BLOCK, LANES),
            shape(1, vectors, kind=jnp.int32),
        ),
        2**31,
        assignment.reshape(1, vectors),
        second_choice.reshape(1, vectors),
        list_slot.reshape(-1, LANES),
        embeddings,
        scratch=[
            pltpu.VMEM((1, vectors), jnp.int32),
            pltpu.VMEM((1, vectors), jnp.int32),
            pltpu.VMEM((list_slot.shape[0] // LANES, LANES), jnp.int32),
            pltpu.VMEM((vectors, width), BF16),
            pltpu.SemaphoreType.DMA((4,)),
        ],
        space=pl.BlockSpec(memory_space=pl.ANY),
        limit=60 * 2**20,
    )
    arrived = exchange(("x", "mem"), payload)
    steps = chips // 2
    near, far, *along = call(
        functools.partial(turn, chips),
        "turn",
        [shape(lists, LANES)] * 2 + [shape(2 * lists, LANES)] * (steps - 1),
        2**20,
        old_centroids,
        across(old_centroids),
        scalars=where,
    )
    olds = [near, lax.ppermute(far, "x", [(i, (i + steps) % chips) for i in range(chips)])]
    for k in range(1, steps):
        pairs = [(2 * i, 2 * ((i + k) % chips)) for i in range(chips)]
        pairs += [(2 * i + 1, 2 * ((i - k) % chips) + 1) for i in range(chips)]
        olds.append(lax.ppermute(along[k - 1], ("x", "core"), pairs))
    arrived, *olds = lax.optimization_barrier((arrived, *olds))
    columns = call(
        functools.partial(gather, capacity),
        "gather",
        shape(chips, slots + NOTES, LANES),
        2**24,
        arrived,
    )
    mine = call(
        functools.partial(sums, groups),
        "sums",
        shape(groups * (LANES + 2), LANES),
        2**32,
        columns,
        *olds,
        scalars=where,
        scratch=[pltpu.VMEM((groups * LANES, 2 * LANES), F32)],
    )
    parts, lists_of = call(
        functools.partial(refit, groups),
        "refit",
        (shape(chips, lists, LANES), shape(groups * LANES, 2 * LANES)),
        2**24,
        mine,
        across(mine),
        scalars=where,
    )
    returned_parts = exchange("x", parts)
    scores = call(
        functools.partial(score, groups),
        "score",
        shape(chips, slots, kind=F32),
        2**33,
        columns,
        lists_of,
    )
    scores, returned_parts = lax.optimization_barrier((scores, returned_parts))
    fresh = returned_parts.swapaxes(0, 1).reshape(lists, width)
    scores = exchange("x", scores.reshape(chips, 1, slots))
    margin = jnp.sum(scores.reshape(chips, slots), axis=0) * (1.0 / width)
    margin = jnp.concatenate(
        [
            margin[: TILE * members].reshape(members, TILE),
            margin[TILE * members : count].reshape(capacity - TILE, members).T,
        ],
        axis=1,
    )
    returned = exchange("mem", margin.reshape(members, 1, capacity))
    spots = jnp.arange(count, dtype=jnp.int32)
    margins = jnp.sum(
        jnp.where(place.reshape(vectors, 1) == spots[None, :], returned.reshape(1, count), 0.0),
        axis=1,
    )
    return fresh, margins


def solution(mesh):
    groups, members = mesh.devices.shape
    chip_mesh = Mesh(mesh.devices.reshape(groups // 2, 2, members), ("x", "core", "mem"))
    everywhere = ("x", "core", "mem")
    placed = (
        P(everywhere, None),
        P(everywhere),
        P(everywhere),
        P(),
        P(everywhere, None),
    )
    return jax.shard_map(
        on_device,
        mesh=chip_mesh,
        in_specs=placed,
        out_specs=(P(everywhere, None), P(everywhere)),
        check_vma=False,
    )
```

```python
import functools

import jax
import jax.numpy as jnp
from jax import lax
from jax.experimental import pallas as pl
from jax.experimental.pallas import tpu as pltpu
from jax.sharding import Mesh
from jax.sharding import PartitionSpec as P

F32 = jnp.float32
BF16 = jnp.bfloat16
LANES = 128
ROWS = 4
WIDE = 3 * LANES
NOTES = 32
LIMIT = 28 * 2**20
SMEM = pl.BlockSpec(memory_space=pltpu.SMEM)
VMEM = pl.BlockSpec(memory_space=pltpu.VMEM)


def rows_of(shape):
    return lax.broadcasted_iota(jnp.int32, shape, 0).astype(F32)


def lanes_of(shape):
    return lax.broadcasted_iota(jnp.int32, shape, 1).astype(F32)


def hot(condition):
    return jnp.where(condition, 1.0, 0.0).astype(BF16)


def dot(a, b, contract):
    return lax.dot_general(a, b, (contract, ((), ())), preferred_element_type=F32)


def whole(a, size):
    return jnp.floor((a + 0.5) * (1.0 / size))


def call(kernel, name, out_shape, flops, *args, scalars=None, scratch=(), space=VMEM, limit=LIMIT):
    specs = [space] * len(args)
    if scalars is not None:
        specs = [SMEM] + specs
        args = (scalars,) + args
    return pl.pallas_call(
        kernel,
        in_specs=specs,
        out_shape=out_shape,
        scratch_shapes=scratch,
        compiler_params=pltpu.CompilerParams(vmem_limit_bytes=limit),
        cost_estimate=pl.CostEstimate(flops=flops, bytes_accessed=2**21, transcendentals=0),
        name=name,
    )(*args)


def prepare(members, capacity, *refs):
    sources, (payload, place), scratch = refs[:4], refs[4:6], refs[6:]
    first, second, table, embeddings, sems = scratch
    copies = [
        pltpu.make_async_copy(source, to, sems.at[n])
        for n, (source, to) in enumerate(zip(sources, scratch))
    ]
    for copy in copies:
        copy.start()
    for copy in copies[:3]:
        copy.wait()
    vectors = first.shape[1]
    slots = table[...]
    local = slots & (LANES - 1)
    owner = (slots // LANES) & (members - 1)
    group = slots // (LANES * members)
    planes = jnp.concatenate([local, owner, group], axis=1).astype(F32).astype(BF16)

    def look_up(ids):
        row = (ids // LANES).astype(F32)
        lane = (ids & (LANES - 1)).astype(F32)
        found = dot(planes, hot(rows_of((table.shape[0], vectors)) == row), ((0,), (0,)))
        mask = rows_of((LANES, vectors)) == lane

        def pick(k):
            return jnp.sum(
                jnp.where(mask, found[k * LANES : (k + 1) * LANES], 0.0), axis=0, keepdims=True
            )

        return pick(0), pick(1), pick(2)

    first_local, first_owner, first_group = look_up(first[...])
    second_local, _, second_group = look_up(second[...])
    is_owner = rows_of((members, vectors)) == first_owner
    before = hot(rows_of((vectors, vectors)) < lanes_of((vectors, vectors)))
    earlier = dot(hot(is_owner), before, ((1,), (0,)))
    rank = jnp.sum(jnp.where(is_owner, earlier, 0.0), axis=0, keepdims=True)
    place[...] = (first_owner * capacity + rank).astype(jnp.int32)
    spot = rank * members + first_owner
    order = hot(rows_of((members * capacity, vectors)) == spot)
    copies[3].wait()
    packed = dot(order, embeddings[...], ((1,), (0,)))
    ranked = rows_of((16, vectors)) == rank
    digits = [first_group + 1.0, first_local, second_group + 1.0, second_local]
    spread = [jnp.where(ranked, digit, 0.0) for digit in digits]
    spread.append(jnp.zeros((LANES - 16 * len(digits), vectors), F32))
    labels = dot(hot(is_owner), jnp.concatenate(spread, axis=0).astype(BF16), ((1,), (1,)))
    empty = [jnp.zeros((members, LANES), F32)] * (ROWS * WIDE // LANES - capacity - 1)
    for j in range(embeddings.shape[1] // LANES):
        at = slice(j * LANES, (j + 1) * LANES)
        rows = [packed[p * members : (p + 1) * members, at] for p in range(capacity)]
        rows += [labels] + empty
        block = [jnp.stack(rows[t : t + ROWS], axis=1) for t in range(0, len(rows), ROWS)]
        payload[j * members : (j + 1) * members] = jnp.concatenate(block, axis=2).astype(BF16)


def gather(capacity, arrived, out):
    chips, rows, _ = out.shape
    members = arrived.shape[0] // chips
    count = members * capacity
    slots = rows - NOTES
    vector = lanes_of((members, slots))
    from_member = vector - members * whole(vector, members)
    from_member = hot(rows_of((members, slots)) == from_member)
    ranked = rows_of((16, slots)) == whole(lanes_of((16, slots)), members)
    for s in range(chips):
        values = arrived[s * members : (s + 1) * members].astype(F32)

        def row(p):
            start = p // ROWS * LANES
            return values[:, p % ROWS, start : start + LANES].astype(BF16)

        for p in range(capacity):
            out[s, p * members : (p + 1) * members] = row(p)
        if slots > count:
            out[s, count:slots] = jnp.zeros((slots - count, LANES), BF16)
        found = dot(row(capacity), from_member, ((0,), (0,)))
        notes = []
        for k in range(4):
            row = jnp.where(ranked, found[k * 16 : (k + 1) * 16], 0.0)
            row = jnp.sum(row, axis=0, keepdims=True)
            notes += [row[:, q : q + LANES] for q in range(0, slots, LANES)]
        notes.append(jnp.zeros((NOTES - len(notes), LANES), F32))
        out[s, slots:] = jnp.concatenate(notes, axis=0).astype(BF16)


def labels_of(slots, notes, k):
    chunks = slots // LANES

    def row(d):
        return jnp.concatenate(
            [notes[d * chunks + q : d * chunks + q + 1] for q in range(chunks)], axis=1
        )

    return row(2 * k) - 1.0, row(2 * k + 1)


def turn(chips, where, old, other, near, far, *along):
    def share(a, chip):
        return a[:, pl.ds(pl.multiple_of(chip * LANES, LANES), LANES)]

    near[...] = share(old, where[0])
    far[...] = share(old, lax.rem(where[0] + chips // 2, chips))
    for k, out in enumerate(along, 1):
        chip = lax.rem(where[0] + chips + (1 - 2 * where[1]) * k, chips)
        one, two = share(old, chip).astype(F32), share(other, chip).astype(F32)
        out[:LANES] = jnp.where(where[1] == 0, one, two).astype(BF16)
        out[LANES:] = jnp.where(where[1] == 0, two, one).astype(BF16)


def bare(wide):
    return jnp.concatenate([wide, jnp.ones(wide.shape, BF16)], axis=1)


def pair_of(columns, slots, t):
    both = [columns[2 * t + n, 0:slots] for n in range(2)]
    notes = [columns[2 * t + n, slots:].astype(F32) for n in range(2)]

    def labels(k):
        found = [labels_of(slots, note, k) for note in notes]
        return (
            jnp.concatenate([found[0][0], found[1][0]], axis=1),
            jnp.concatenate([found[0][1], found[1][1]], axis=1),
        )

    return bare(jnp.concatenate(both, axis=0)), labels


def sums(groups, where, columns, *refs):
    olds, (out, total) = refs[:-2], refs[-2:]
    chips, rows, _ = columns.shape
    slots = rows - NOTES
    total[...] = jnp.zeros(total.shape, F32)

    def step(t, _):
        vectors, labels = pair_of(columns, slots, t)
        group, local = labels(0)
        at = hot(rows_of((LANES, 2 * slots)) == local)
        table = jnp.concatenate([at * hot(group == float(g)) for g in range(groups)], axis=0)
        total[...] += dot(table, vectors, ((1,), (0,)))
        return 0

    lax.fori_loop(0, chips // 2, step, 0)
    identity = rows_of((LANES, LANES)) == lanes_of((LANES, LANES))
    counts = []
    for g in range(groups):
        at = slice(g * LANES, (g + 1) * LANES)
        counts.append(
            jnp.sum(jnp.where(identity, total[at, LANES:], 0.0), axis=0, keepdims=True)
        )
    near, far, *along = olds
    for old, chip in ((near, where[0]), (far, lax.rem(where[0] + chips // 2, chips))):
        at = pl.ds(pl.multiple_of((2 * chip + where[1]) * LANES, LANES), LANES)
        total[at, :LANES] += old[...].astype(F32)
    for k, old in enumerate(along, 1):
        chip = lax.rem(where[0] + chips - (1 - 2 * where[1]) * k, chips)
        at = pl.ds(pl.multiple_of(2 * chip * LANES, 2 * LANES), 2 * LANES)
        total[at, :LANES] += old[...].astype(F32)
    out[: groups * LANES] = total[:, :LANES].astype(BF16)
    counts = jnp.concatenate(counts, axis=0)
    high = whole(counts, 256)
    out[groups * LANES : groups * (LANES + 1)] = (counts - 256.0 * high).astype(BF16)
    out[groups * (LANES + 1) :] = high.astype(BF16)


def refit(groups, where, mine, theirs, parts, lists_of):
    lists = groups * LANES

    def counts_of(sums):
        low = sums[lists : lists + groups].astype(F32)
        return low + 256.0 * sums[lists + groups :].astype(F32)

    counts = counts_of(mine) + counts_of(theirs) + 1.0
    identity = rows_of((LANES, LANES)) == lanes_of((LANES, LANES))
    lane = lanes_of((LANES, LANES))
    values = []
    for g in range(groups):
        at = slice(g * LANES, (g + 1) * LANES)
        divisor = jnp.sum(jnp.where(identity, counts[g : g + 1], 0.0), axis=1, keepdims=True)
        total = mine[at].astype(F32) + theirs[at].astype(F32)
        value = (total / divisor).astype(BF16).astype(F32)
        values.append(value)
        size = jnp.sum(value * value, axis=1, keepdims=True)
        one = size.astype(BF16).astype(F32)
        two = (size - one).astype(BF16).astype(F32)
        three = size - one - two
        sizes = jnp.where(lane == 0.0, one, jnp.where(lane == 1.0, two, 0.0))
        sizes = jnp.where(lane == 2.0, three, sizes)
        lists_of[at] = jnp.concatenate([-2.0 * value, sizes], axis=1).astype(BF16)
    for s in range(groups // 2):
        parts[s] = jnp.where(where[1] == 0, values[2 * s], values[2 * s + 1]).astype(BF16)


def score(groups, columns, lists_of, margins):
    chips, rows, _ = columns.shape
    slots = rows - NOTES

    def step(t, _):
        vectors, labels = pair_of(columns, slots, t)
        distance = dot(lists_of[...], vectors, ((1,), (1,)))

        def pick(k):
            group, local = labels(k)
            found = jnp.zeros((LANES, 2 * slots), F32)
            for g in range(groups):
                found = jnp.where(
                    group == float(g), distance[g * LANES : (g + 1) * LANES], found
                )
            return jnp.where(rows_of((LANES, 2 * slots)) == local, found, 0.0)

        margin = jnp.sum(pick(1) - pick(0), axis=0, keepdims=True)
        margins[pl.ds(2 * t, 1), :] = margin[:, :slots]
        margins[pl.ds(2 * t + 1, 1), :] = margin[:, slots:]
        return 0

    lax.fori_loop(0, chips // 2, step, 0)


def on_device(embeddings, assignment, second_choice, list_slot, old_centroids):
    vectors, width = embeddings.shape
    lists = old_centroids.shape[0]
    members = lax.axis_size("mem")
    chips = lax.axis_size("x")
    capacity = vectors // members + 2
    count = members * capacity

    groups = 2 * chips
    slots = count + -count % LANES

    def across(a):
        return lax.ppermute(a, "core", [(0, 1), (1, 0)])

    def shape(*dims, kind=BF16):
        return jax.ShapeDtypeStruct(dims, kind)

    def exchange(axis, a):
        return lax.all_to_all(a, axis, split_axis=0, concat_axis=0, tiled=True)

    where = jnp.stack([lax.axis_index("x"), lax.axis_index("core")]).astype(jnp.int32)
    payload, place = call(
        functools.partial(prepare, members, capacity),
        "prepare",
        (
            shape(chips * members, ROWS, WIDE),
            shape(1, vectors, kind=jnp.int32),
        ),
        2**31,
        assignment.reshape(1, vectors),
        second_choice.reshape(1, vectors),
        list_slot.reshape(-1, LANES),
        embeddings,
        scratch=[
            pltpu.VMEM((1, vectors), jnp.int32),
            pltpu.VMEM((1, vectors), jnp.int32),
            pltpu.VMEM((list_slot.shape[0] // LANES, LANES), jnp.int32),
            pltpu.VMEM((vectors, width), BF16),
            pltpu.SemaphoreType.DMA((4,)),
        ],
        space=pl.BlockSpec(memory_space=pl.ANY),
        limit=60 * 2**20,
    )
    arrived = exchange(("x", "mem"), payload)
    steps = chips // 2
    near, far, *along = call(
        functools.partial(turn, chips),
        "turn",
        [shape(lists, LANES)] * 2 + [shape(2 * lists, LANES)] * (steps - 1),
        2**20,
        old_centroids,
        across(old_centroids),
        scalars=where,
    )
    olds = [near, lax.ppermute(far, "x", [(i, (i + steps) % chips) for i in range(chips)])]
    for k in range(1, steps):
        pairs = [(2 * i, 2 * ((i + k) % chips)) for i in range(chips)]
        pairs += [(2 * i + 1, 2 * ((i - k) % chips) + 1) for i in range(chips)]
        olds.append(lax.ppermute(along[k - 1], ("x", "core"), pairs))
    arrived, *olds = lax.optimization_barrier((arrived, *olds))
    columns = call(
        functools.partial(gather, capacity),
        "gather",
        shape(chips, slots + NOTES, LANES),
        2**24,
        arrived,
    )
    mine = call(
        functools.partial(sums, groups),
        "sums",
        shape(groups * (LANES + 2), LANES),
        2**32,
        columns,
        *olds,
        scalars=where,
        scratch=[pltpu.VMEM((groups * LANES, 2 * LANES), F32)],
    )
    parts, lists_of = call(
        functools.partial(refit, groups),
        "refit",
        (shape(chips, lists, LANES), shape(groups * LANES, 2 * LANES)),
        2**24,
        mine,
        across(mine),
        scalars=where,
    )
    returned_parts = exchange("x", parts)
    scores = call(
        functools.partial(score, groups),
        "score",
        shape(chips, slots, kind=F32),
        2**33,
        columns,
        lists_of,
    )
    scores, returned_parts = lax.optimization_barrier((scores, returned_parts))
    fresh = returned_parts.swapaxes(0, 1).reshape(lists, width)
    scores = exchange("x", scores.reshape(chips, 1, slots))
    margin = jnp.sum(scores.reshape(chips, slots), axis=0) * (1.0 / width)
    margin = margin[:count].reshape(capacity, members).T
    returned = exchange("mem", margin.reshape(members, 1, capacity))
    spots = jnp.arange(count, dtype=jnp.int32)
    margins = jnp.sum(
        jnp.where(place.reshape(vectors, 1) == spots[None, :], returned.reshape(1, count), 0.0),
        axis=1,
    )
    return fresh, margins


def solution(mesh):
    groups, members = mesh.devices.shape
    chip_mesh = Mesh(mesh.devices.reshape(groups // 2, 2, members), ("x", "core", "mem"))
    everywhere = ("x", "core", "mem")
    placed = (
        P(everywhere, None),
        P(everywhere),
        P(everywhere),
        P(),
        P(everywhere, None),
    )
    return jax.shard_map(
        on_device,
        mesh=chip_mesh,
        in_specs=placed,
        out_specs=(P(everywhere, None), P(everywhere)),
        check_vma=False,
    )
```

```python
import functools

import jax
import jax.numpy as jnp
from jax import lax
from jax.experimental import pallas as pl
from jax.experimental.pallas import tpu as pltpu
from jax.sharding import Mesh
from jax.sharding import PartitionSpec as P

F32 = jnp.float32
BF16 = jnp.bfloat16
LANES = 128
ROWS = 4
FULL = 8
WIDE = 3 * LANES
NOTES = 32
LIMIT = 28 * 2**20
SMEM = pl.BlockSpec(memory_space=pltpu.SMEM)
VMEM = pl.BlockSpec(memory_space=pltpu.VMEM)


def rows_of(shape):
    return lax.broadcasted_iota(jnp.int32, shape, 0).astype(F32)


def lanes_of(shape):
    return lax.broadcasted_iota(jnp.int32, shape, 1).astype(F32)


def hot(condition):
    return jnp.where(condition, 1.0, 0.0).astype(BF16)


def dot(a, b, contract):
    return lax.dot_general(a, b, (contract, ((), ())), preferred_element_type=F32)


def whole(a, size):
    return jnp.floor((a + 0.5) * (1.0 / size))


def call(kernel, name, out_shape, flops, *args, scalars=None, scratch=(), space=VMEM, limit=LIMIT):
    specs = [space] * len(args)
    if scalars is not None:
        specs = [SMEM] + specs
        args = (scalars,) + args
    return pl.pallas_call(
        kernel,
        in_specs=specs,
        out_shape=out_shape,
        scratch_shapes=scratch,
        compiler_params=pltpu.CompilerParams(vmem_limit_bytes=limit),
        cost_estimate=pl.CostEstimate(flops=flops, bytes_accessed=2**21, transcendentals=0),
        name=name,
    )(*args)


def prepare(members, capacity, *refs):
    sources, (payload, place), scratch = refs[:4], refs[4:6], refs[6:]
    first, second, table, embeddings, sems = scratch
    copies = [
        pltpu.make_async_copy(source, to, sems.at[n])
        for n, (source, to) in enumerate(zip(sources, scratch))
    ]
    for copy in copies:
        copy.start()
    for copy in copies[:3]:
        copy.wait()
    vectors = first.shape[1]
    slots = table[...]
    local = slots & (LANES - 1)
    owner = (slots // LANES) & (members - 1)
    group = slots // (LANES * members)
    planes = jnp.concatenate([local, owner, group], axis=1).astype(F32).astype(BF16)

    def look_up(ids):
        row = (ids // LANES).astype(F32)
        lane = (ids & (LANES - 1)).astype(F32)
        found = dot(planes, hot(rows_of((table.shape[0], vectors)) == row), ((0,), (0,)))
        mask = rows_of((LANES, vectors)) == lane

        def pick(k):
            return jnp.sum(
                jnp.where(mask, found[k * LANES : (k + 1) * LANES], 0.0), axis=0, keepdims=True
            )

        return pick(0), pick(1), pick(2)

    first_local, first_owner, first_group = look_up(first[...])
    second_local, _, second_group = look_up(second[...])
    is_owner = rows_of((members, vectors)) == first_owner
    before = hot(rows_of((vectors, vectors)) < lanes_of((vectors, vectors)))
    earlier = dot(hot(is_owner), before, ((1,), (0,)))
    rank = jnp.sum(jnp.where(is_owner, earlier, 0.0), axis=0, keepdims=True)
    place[...] = (first_owner * capacity + rank).astype(jnp.int32)
    turn_of = whole(rank, ROWS)
    spot = (turn_of * members + first_owner) * ROWS + rank - ROWS * turn_of
    spot = jnp.where(rank < FULL, spot, rank * members + first_owner)
    order = hot(rows_of((members * capacity, vectors)) == spot)
    copies[3].wait()
    packed = dot(order, embeddings[...], ((1,), (0,)))
    ranked = rows_of((16, vectors)) == rank
    digits = [first_group + 1.0, first_local, second_group + 1.0, second_local]
    spread = [jnp.where(ranked, digit, 0.0) for digit in digits]
    spread.append(jnp.zeros((LANES - 16 * len(digits), vectors), F32))
    labels = dot(hot(is_owner), jnp.concatenate(spread, axis=0).astype(BF16), ((1,), (1,)))
    empty = [jnp.zeros((members, LANES), F32)] * (ROWS * WIDE // LANES - capacity - 1)
    for j in range(embeddings.shape[1] // LANES):
        at = slice(j * LANES, (j + 1) * LANES)
        rows = [packed[p * members : (p + 1) * members, at] for p in range(FULL, capacity)]
        rows += [labels] + empty
        block = [
            packed[p * members : (p + ROWS) * members, at].reshape(members, ROWS, LANES)
            for p in range(0, FULL, ROWS)
        ]
        block.append(jnp.stack(rows, axis=1))
        payload[j * members : (j + 1) * members] = jnp.concatenate(block, axis=2).astype(BF16)


def gather(capacity, arrived, out):
    chips, rows, _ = out.shape
    members = arrived.shape[0] // chips
    count = members * capacity
    slots = rows - NOTES
    vector = lanes_of((members, slots))
    quarter = whole(vector, ROWS)
    quarter = jnp.where(vector < FULL * members, quarter, vector)
    from_member = hot(
        rows_of((members, slots)) == quarter - members * whole(quarter, members)
    )
    vector = lanes_of((16, slots))
    quarter = whole(vector, ROWS)
    rank = ROWS * whole(quarter, members) + vector - ROWS * quarter
    rank = jnp.where(vector < FULL * members, rank, whole(vector, members))
    ranked = rows_of((16, slots)) == rank
    for s in range(chips):
        values = arrived[s * members : (s + 1) * members].astype(F32)

        def row(p):
            start = p // ROWS * LANES
            return values[:, p % ROWS, start : start + LANES].astype(BF16)

        for t in range(FULL // ROWS):
            full = values[:, :, t * LANES : (t + 1) * LANES].reshape(ROWS * members, LANES)
            out[s, t * ROWS * members : (t + 1) * ROWS * members] = full.astype(BF16)
        for p in range(FULL, capacity):
            out[s, p * members : (p + 1) * members] = row(p)
        if slots > count:
            out[s, count:slots] = jnp.zeros((slots - count, LANES), BF16)
        found = dot(row(capacity), from_member, ((0,), (0,)))
        notes = []
        for k in range(4):
            row = jnp.where(ranked, found[k * 16 : (k + 1) * 16], 0.0)
            row = jnp.sum(row, axis=0, keepdims=True)
            notes += [row[:, q : q + LANES] for q in range(0, slots, LANES)]
        notes.append(jnp.zeros((NOTES - len(notes), LANES), F32))
        out[s, slots:] = jnp.concatenate(notes, axis=0).astype(BF16)


def labels_of(slots, notes, k):
    chunks = slots // LANES

    def row(d):
        return jnp.concatenate(
            [notes[d * chunks + q : d * chunks + q + 1] for q in range(chunks)], axis=1
        )

    return row(2 * k) - 1.0, row(2 * k + 1)


def turn(chips, where, old, other, near, far, *along):
    def share(a, chip):
        return a[:, pl.ds(pl.multiple_of(chip * LANES, LANES), LANES)]

    near[...] = share(old, where[0])
    far[...] = share(old, lax.rem(where[0] + chips // 2, chips))
    for k, out in enumerate(along, 1):
        chip = lax.rem(where[0] + chips + (1 - 2 * where[1]) * k, chips)
        one, two = share(old, chip).astype(F32), share(other, chip).astype(F32)
        out[:LANES] = jnp.where(where[1] == 0, one, two).astype(BF16)
        out[LANES:] = jnp.where(where[1] == 0, two, one).astype(BF16)


def bare(wide):
    return jnp.concatenate([wide, jnp.ones(wide.shape, BF16)], axis=1)


def pair_of(columns, slots, t):
    both = [columns[2 * t + n, 0:slots] for n in range(2)]
    notes = [columns[2 * t + n, slots:].astype(F32) for n in range(2)]

    def labels(k):
        found = [labels_of(slots, note, k) for note in notes]
        return (
            jnp.concatenate([found[0][0], found[1][0]], axis=1),
            jnp.concatenate([found[0][1], found[1][1]], axis=1),
        )

    return bare(jnp.concatenate(both, axis=0)), labels


def sums(groups, where, columns, *refs):
    olds, (out, total) = refs[:-2], refs[-2:]
    chips, rows, _ = columns.shape
    slots = rows - NOTES
    total[...] = jnp.zeros(total.shape, F32)

    def step(t, _):
        vectors, labels = pair_of(columns, slots, t)
        group, local = labels(0)
        at = hot(rows_of((LANES, 2 * slots)) == local)
        table = jnp.concatenate([at * hot(group == float(g)) for g in range(groups)], axis=0)
        total[...] += dot(table, vectors, ((1,), (0,)))
        return 0

    lax.fori_loop(0, chips // 2, step, 0)
    identity = rows_of((LANES, LANES)) == lanes_of((LANES, LANES))
    counts = []
    for g in range(groups):
        at = slice(g * LANES, (g + 1) * LANES)
        counts.append(
            jnp.sum(jnp.where(identity, total[at, LANES:], 0.0), axis=0, keepdims=True)
        )
    near, far, *along = olds
    for old, chip in ((near, where[0]), (far, lax.rem(where[0] + chips // 2, chips))):
        at = pl.ds(pl.multiple_of((2 * chip + where[1]) * LANES, LANES), LANES)
        total[at, :LANES] += old[...].astype(F32)
    for k, old in enumerate(along, 1):
        chip = lax.rem(where[0] + chips - (1 - 2 * where[1]) * k, chips)
        at = pl.ds(pl.multiple_of(2 * chip * LANES, 2 * LANES), 2 * LANES)
        total[at, :LANES] += old[...].astype(F32)
    out[: groups * LANES] = total[:, :LANES].astype(BF16)
    counts = jnp.concatenate(counts, axis=0)
    high = whole(counts, 256)
    out[groups * LANES : groups * (LANES + 1)] = (counts - 256.0 * high).astype(BF16)
    out[groups * (LANES + 1) :] = high.astype(BF16)


def refit(groups, where, mine, theirs, parts, lists_of):
    lists = groups * LANES

    def counts_of(sums):
        low = sums[lists : lists + groups].astype(F32)
        return low + 256.0 * sums[lists + groups :].astype(F32)

    counts = counts_of(mine) + counts_of(theirs) + 1.0
    identity = rows_of((LANES, LANES)) == lanes_of((LANES, LANES))
    values = []
    for g in range(groups):
        at = slice(g * LANES, (g + 1) * LANES)
        divisor = jnp.sum(jnp.where(identity, counts[g : g + 1], 0.0), axis=1, keepdims=True)
        total = mine[at].astype(F32) + theirs[at].astype(F32)
        value = (total / divisor).astype(BF16)
        values.append(value)
        lists_of[at] = value
    for s in range(groups // 2):
        one, two = values[2 * s].astype(F32), values[2 * s + 1].astype(F32)
        parts[s] = jnp.where(where[1] == 0, one, two).astype(BF16)


def score(groups, columns, fresh, margins, lists_of):
    chips, rows, _ = columns.shape
    slots = rows - NOTES
    lane = lanes_of((LANES, LANES))
    for g in range(groups):
        at = slice(g * LANES, (g + 1) * LANES)
        value = fresh[at].astype(F32)
        size = jnp.sum(value * value, axis=1, keepdims=True)
        one = size.astype(BF16).astype(F32)
        two = (size - one).astype(BF16).astype(F32)
        three = size - one - two
        sizes = jnp.where(lane == 0.0, one, jnp.where(lane == 1.0, two, 0.0))
        sizes = jnp.where(lane == 2.0, three, sizes)
        lists_of[at] = jnp.concatenate([-2.0 * value, sizes], axis=1).astype(BF16)

    def step(t, _):
        vectors, labels = pair_of(columns, slots, t)
        distance = dot(lists_of[...], vectors, ((1,), (1,)))

        def pick(k):
            group, local = labels(k)
            found = jnp.zeros((LANES, 2 * slots), F32)
            for g in range(groups):
                found = jnp.where(
                    group == float(g), distance[g * LANES : (g + 1) * LANES], found
                )
            return jnp.where(rows_of((LANES, 2 * slots)) == local, found, 0.0)

        margin = jnp.sum(pick(1) - pick(0), axis=0, keepdims=True)
        margins[pl.ds(2 * t, 1), :] = margin[:, :slots]
        margins[pl.ds(2 * t + 1, 1), :] = margin[:, slots:]
        return 0

    lax.fori_loop(0, chips // 2, step, 0)


def on_device(embeddings, assignment, second_choice, list_slot, old_centroids):
    vectors, width = embeddings.shape
    lists = old_centroids.shape[0]
    members = lax.axis_size("mem")
    chips = lax.axis_size("x")
    capacity = vectors // members + 2
    count = members * capacity

    groups = 2 * chips
    slots = count + -count % LANES

    def across(a):
        return lax.ppermute(a, "core", [(0, 1), (1, 0)])

    def shape(*dims, kind=BF16):
        return jax.ShapeDtypeStruct(dims, kind)

    def exchange(axis, a):
        return lax.all_to_all(a, axis, split_axis=0, concat_axis=0, tiled=True)

    where = jnp.stack([lax.axis_index("x"), lax.axis_index("core")]).astype(jnp.int32)
    payload, place = call(
        functools.partial(prepare, members, capacity),
        "prepare",
        (
            shape(chips * members, ROWS, WIDE),
            shape(1, vectors, kind=jnp.int32),
        ),
        2**31,
        assignment.reshape(1, vectors),
        second_choice.reshape(1, vectors),
        list_slot.reshape(-1, LANES),
        embeddings,
        scratch=[
            pltpu.VMEM((1, vectors), jnp.int32),
            pltpu.VMEM((1, vectors), jnp.int32),
            pltpu.VMEM((list_slot.shape[0] // LANES, LANES), jnp.int32),
            pltpu.VMEM((vectors, width), BF16),
            pltpu.SemaphoreType.DMA((4,)),
        ],
        space=pl.BlockSpec(memory_space=pl.ANY),
        limit=60 * 2**20,
    )
    arrived = exchange(("x", "mem"), payload)
    steps = chips // 2
    near, far, *along = call(
        functools.partial(turn, chips),
        "turn",
        [shape(lists, LANES)] * 2 + [shape(2 * lists, LANES)] * (steps - 1),
        2**20,
        old_centroids,
        across(old_centroids),
        scalars=where,
    )
    olds = [near, lax.ppermute(far, "x", [(i, (i + steps) % chips) for i in range(chips)])]
    for k in range(1, steps):
        pairs = [(2 * i, 2 * ((i + k) % chips)) for i in range(chips)]
        pairs += [(2 * i + 1, 2 * ((i - k) % chips) + 1) for i in range(chips)]
        olds.append(lax.ppermute(along[k - 1], ("x", "core"), pairs))
    arrived, *olds = lax.optimization_barrier((arrived, *olds))
    columns = call(
        functools.partial(gather, capacity),
        "gather",
        shape(chips, slots + NOTES, LANES),
        2**24,
        arrived,
    )
    mine = call(
        functools.partial(sums, groups),
        "sums",
        shape(groups * (LANES + 2), LANES),
        2**32,
        columns,
        *olds,
        scalars=where,
        scratch=[pltpu.VMEM((groups * LANES, 2 * LANES), F32)],
    )
    parts, lists_of = call(
        functools.partial(refit, groups),
        "refit",
        (shape(chips, lists, LANES), shape(groups * LANES, LANES)),
        2**24,
        mine,
        across(mine),
        scalars=where,
    )
    returned_parts = exchange("x", parts)
    scores = call(
        functools.partial(score, groups),
        "score",
        shape(chips, slots, kind=F32),
        2**33,
        columns,
        lists_of,
        scratch=[pltpu.VMEM((groups * LANES, 2 * LANES), BF16)],
    )
    scores, returned_parts = lax.optimization_barrier((scores, returned_parts))
    fresh = returned_parts.swapaxes(0, 1).reshape(lists, width)
    scores = exchange("x", scores.reshape(chips, 1, slots))
    margin = jnp.sum(scores.reshape(chips, slots), axis=0) * (1.0 / width)
    full = margin[: FULL * members].reshape(FULL // ROWS, members, ROWS)
    rest = margin[FULL * members : count].reshape(capacity - FULL, members)
    margin = jnp.concatenate([full.swapaxes(0, 1).reshape(members, FULL), rest.T], axis=1)
    returned = exchange("mem", margin.reshape(members, 1, capacity))
    spots = jnp.arange(count, dtype=jnp.int32)
    margins = jnp.sum(
        jnp.where(place.reshape(vectors, 1) == spots[None, :], returned.reshape(1, count), 0.0),
        axis=1,
    )
    return fresh, margins


def solution(mesh):
    groups, members = mesh.devices.shape
    chip_mesh = Mesh(mesh.devices.reshape(groups // 2, 2, members), ("x", "core", "mem"))
    everywhere = ("x", "core", "mem")
    placed = (
        P(everywhere, None),
        P(everywhere),
        P(everywhere),
        P(),
        P(everywhere, None),
    )
    return jax.shard_map(
        on_device,
        mesh=chip_mesh,
        in_specs=placed,
        out_specs=(P(everywhere, None), P(everywhere)),
        check_vma=False,
    )
```
